256 devices in a mesh: group: 2 (over z_hi), dp: 8 (over x, core), tensor: 16 (over z_lo, y).
Axes of the slice: x: 4, y: 4, z: 8 (z_hi: 2, z_lo: 4; z = z_hi * 4 + z_lo), core: 2. Of those that a mesh axis runs over, the one named last changes fastest.
Arguments:
- teacher_hidden: bfloat16 [4096, 8192], P(('group', 'dp'), 'tensor'), may hold values from -6 to 6
- teacher_gain: float32 [8192], P('tensor'), may hold values from 0.1 to 1.9
- project_weight: bfloat16 [8192, 3584], P('tensor'), may hold values from -0.0625 to 0.0625
- student_hidden: bfloat16 [4096, 3584], P(('group', 'dp', 'tensor')), may hold values from -6 to 6
- student_gain: float32 [3584], replicated, may hold values from 0.1 to 1.9
- gate_weight: bfloat16 [3584, 9472], P(('group', 'dp'), 'tensor'), may hold values from -0.09375 to 0.09375
- up_weight: bfloat16 [3584, 9472], P(('group', 'dp'), 'tensor'), may hold values from -0.09375 to 0.09375
- down_weight: bfloat16 [9472, 3584], P('tensor', ('group', 'dp')), may hold values from -0.0625 to 0.0625
- owner_map: int32 [256, 1], P(('group', 'dp')), may hold values from 0 to 15; in each aligned block of 16 rows (0 to 15, 16 to 31, ...) at most 2 rows name the same one
- token_ids: int32 [4096], P(('group', 'dp', 'tensor')), may hold values from 0 to 511
- token_counts: int32 [256], P(('group', 'dp')), may hold values from 1 to 16
- id_weight: float32 [512], replicated, may hold values from 0.25 to 4
Outputs:
- student_out: bfloat16 [16, 16, 32, 3584], P(('group', 'dp'), 'tensor')
- down_grad: float32 [3584, 9472], P(('group', 'dp'), 'tensor')
The draws below stay inside these ranges and needn't reach their ends.
Inputs may be any that keep to these rules, and one draw needn't show every extreme that they name: `owner_map`: of the 16 episodes of one index of group and dp (aligned blocks of 16 rows), at most 2 have the same owner; owner o is index o of group and dp in mesh order.
All inputs are finite; a program needn't handle non-finite values.
Results may differ from the reference program's by a relative error of at most 0.02.
Values may be sent and summed in bfloat16 or wider, within the bound.
No kernel may reach another device: no remote copies, remote signals or barrier semaphores. Data moves between devices by JAX's collectives and lax.ppermute only.
A program may use at most 128 MiB of HBM per device.

```python
import math
import jax
import jax.numpy as jnp
import numpy as np
from jax import lax

DT = 8192
DS = 3584
FSW = 9472
REL_VOCAB = 512
EP_LEN = 16
EPI_DEV = 16
SLOTS = 16
EPISODES = 256
TOKENS = 4096
CAP = 2
RECV = 32
N_GROUP = 2
N_DP = 8
N_TENSOR = 16


def set_ends(values, own_key, low, high):
    longest = values.shape.index(max(values.shape))
    spots = []
    for shift in (0, 1):
        where = [jax.random.randint(jax.random.fold_in(own_key, axis), (), 0, length) for axis, length in enumerate(values.shape)]
        where[longest] = (where[longest] + shift) % values.shape[longest]
        spots.append(tuple(where))
    return values.at[spots[0]].set(low).at[spots[1]].set(high)


def level_of(rng, shape, split, least, largest):
    level, own = 1.0, jax.random.fold_in(rng, 6)
    for dim, blocks in split:
        draws = jnp.exp(jax.random.uniform(jax.random.fold_in(own, dim), (blocks,), jnp.float32, least / len(split), largest / len(split)))
        level = level * jnp.repeat(draws, shape[dim] // blocks).reshape([-1 if axis == dim else 1 for axis in range(len(shape))])
    return level


def rank_table(number_of, lean):
    weights = [(1 << 20) // math.isqrt(rank ** lean) + 1 for rank in range(1, number_of + 1)]
    scale = 1 + sum(weights) // (1 << 30)
    return np.cumsum(np.array([max(1, weight // scale) for weight in weights]))


def ranked(key, shape, amount, skew):
    table = rank_table(amount, skew)
    pick = jax.random.randint(jax.random.fold_in(key, 1), shape, 0, int(table[amount - 1]))
    rank = jnp.searchsorted(jnp.asarray(table, jnp.int32), pick, side="right")
    return jax.random.permutation(jax.random.fold_in(key, 2), amount)[rank].astype(jnp.int32)


def assign_block(stream_key, own, number, rows, amount, top, most, skew):
    ranking = jax.random.permutation(stream_key, amount)
    crowded, usual = portions_of(amount, rows * top, most, skew, True), portions_of(amount, rows * top, most, skew, False)
    places = jnp.arange(amount)

    def named(sizes, rotation):
        used = int((sizes > 0).sum())
        fixed = max(1, used // 4)
        passed = fixed + (places - fixed + rotation * (used - fixed)) % max(1, amount - fixed)
        return jnp.zeros((amount,), jnp.int32).at[ranking[jnp.where(places < fixed, places, passed)]].set(jnp.asarray(sizes, jnp.int32))

    sizes = jnp.where(number % 4 == 0, named(crowded, number // 4), named(usual, number - number // 4 - 1))
    mixed = jax.random.permutation(jax.random.fold_in(own, 3), amount)
    donor, taker = mixed[0:amount // 2 * 2:2], mixed[1:amount // 2 * 2:2]
    margin = jnp.minimum(sizes[donor] - 1, most - sizes[taker]) // 2
    margin = jnp.where((donor == ranking[0]) | (taker == ranking[0]) | (sizes[taker] == 0), 0, jnp.maximum(margin, 0))
    passed = jax.random.randint(jax.random.fold_in(own, 4), (amount // 2,), 0, 1 << 20) % (margin + 1)
    sizes = sizes.at[donor].add(-passed).at[taker].add(passed)
    members = jnp.searchsorted(jnp.cumsum(sizes), jnp.arange(rows * top), side="right").astype(jnp.int32)
    grid = members.reshape(top, rows).T
    grid = grid[jax.random.permutation(jax.random.fold_in(own, 1), rows)]
    rotation = jax.random.randint(jax.random.fold_in(own, 2), (rows, 1), 0, top)
    return jnp.take_along_axis(grid, (jnp.arange(top)[None, :] + rotation) % top, axis=1)


def portions_of(amount, total, limit, lean, full):
    weights = [(1 << 20) // math.isqrt(grade ** lean) + 1 for grade in range(1, amount + 1)]
    largest = limit if full else min(limit, max(-(-total // amount), total * weights[0] // sum(weights)))
    least = 1 if total - largest >= amount - 1 else 0
    given, spare = [largest] + [least] * (amount - 1), total - largest - least * (amount - 1)
    while spare > 0:
        movable = [i for i in range(1, amount) if given[i] < largest] or [i for i in range(1, amount) if given[i] < limit]
        pool, remaining = sum([weights[i] for i in movable]), spare
        for i in movable:
            more = min(limit - given[i], max(1, remaining * weights[i] // pool), spare)
            given[i] = given[i] + more
            spare = spare - more
    return np.array(given)


def centred(own_key, shape, spread, reach, cuts=(), held_as=jnp.bfloat16):
    entries = spread * jax.random.normal(own_key, shape, jnp.float32)
    if cuts:
        entries = entries * level_of(own_key, shape, cuts, -0.22, 0.18)
    return jnp.clip(entries, -reach, reach).astype(held_as)


def setup_inputs(seed: int = 0) -> dict:
    streams_of = jax.random.split(jax.random.key(seed), 13)
    teacher_hidden = centred(streams_of[0], (TOKENS, DT), 1.0, 6.0, ((0, 16), (1, 16)))
    teacher_gain = jnp.clip(1.0 + 0.18 * jax.random.normal(streams_of[1], (DT,), jnp.float32), 0.1, 1.9)
    project_weight = centred(streams_of[2], (DT, DS), DT ** -0.5, 0.0625, ((0, 16),))
    student_hidden = centred(streams_of[3], (TOKENS, DS), 1.0, 6.0, ((0, 256),))
    student_gain = jnp.clip(1.0 + 0.18 * jax.random.normal(streams_of[4], (DS,), jnp.float32), 0.1, 1.9)
    gate_weight = centred(streams_of[5], (DS, FSW), DS ** -0.5, 0.09375, ((0, 16), (1, 16)))
    up_weight = centred(streams_of[6], (DS, FSW), DS ** -0.5, 0.09375, ((0, 16), (1, 16)))
    down_weight = centred(streams_of[7], (FSW, DS), FSW ** -0.5, 0.0625, ((0, 16), (1, 16)))
    owner_map_keys = jax.random.split(jax.random.fold_in(streams_of[8], 1), EPISODES // EPI_DEV)
    owner_map_turns = jax.random.permutation(jax.random.fold_in(streams_of[8], 3), EPISODES // EPI_DEV)
    owner_map = jax.vmap(lambda own, number: assign_block(jax.random.fold_in(streams_of[8], 2), own, number, EPI_DEV, SLOTS, 1, CAP, 2))(owner_map_keys, owner_map_turns).reshape((EPISODES, 1))
    token_ids = set_ends(ranked(streams_of[9], (TOKENS,), REL_VOCAB, 2), jax.random.fold_in(streams_of[9], 3), 0, REL_VOCAB - 1).astype(jnp.int32)
    token_counts = set_ends(jax.random.randint(streams_of[10], (EPISODES,), 1, EP_LEN + 1), jax.random.fold_in(streams_of[10], 1), 1, EP_LEN).astype(jnp.int32)
    id_weight = jnp.clip(jnp.exp(jax.random.uniform(streams_of[11], (REL_VOCAB,), jnp.float32, math.log(0.25), math.log(4.0))), 0.25, 4.0)
    return dict(teacher_hidden=teacher_hidden, teacher_gain=teacher_gain, project_weight=project_weight, student_hidden=student_hidden, student_gain=student_gain, gate_weight=gate_weight, up_weight=up_weight, down_weight=down_weight, owner_map=owner_map, token_ids=token_ids, token_counts=token_counts, id_weight=id_weight)


EPSILON = 1e-06

def reference(teacher_hidden, teacher_gain, project_weight, student_hidden, student_gain, gate_weight, up_weight, down_weight, owner_map, token_ids, token_counts, id_weight):
    owners = N_GROUP * N_DP
    token_index = jnp.arange(TOKENS, dtype=jnp.int32)
    position = token_index // EPI_DEV % EP_LEN
    episode = token_index // (EP_LEN * EPI_DEV) * EPI_DEV + token_index % EPI_DEV
    token_weight = jnp.where(position < token_counts[episode], id_weight[token_ids], 0.0).astype(jnp.bfloat16)
    widened = teacher_hidden.astype(jnp.float32)
    inverse = lax.rsqrt(lax.optimization_barrier(jnp.mean(widened * widened, axis=1)) + EPSILON)
    scaled = (widened * teacher_gain[None, :]).astype(jnp.bfloat16)
    feature_block = DT // N_TENSOR

    def add_teacher(index, total):
        offset = (index * feature_block).astype(jnp.int32)
        columns = lax.dynamic_slice_in_dim(scaled, offset, feature_block, 1)
        weight_rows = lax.dynamic_slice_in_dim(project_weight, offset, feature_block, 0)
        partial_sum = jnp.dot(columns, weight_rows, preferred_element_type=jnp.float32).astype(jnp.bfloat16)
        return total + lax.optimization_barrier(partial_sum).astype(jnp.float32)
    summed = lax.fori_loop(0, N_TENSOR, add_teacher, jnp.zeros((TOKENS, DS), jnp.float32))
    projected = (summed * inverse[:, None]).astype(jnp.bfloat16)
    student_wide = student_hidden.astype(jnp.float32)
    rescale = lax.rsqrt(lax.optimization_barrier(jnp.mean(student_wide * student_wide, axis=1, keepdims=True)) + EPSILON)
    normed = (student_wide * rescale * student_gain[None, :]).astype(jnp.bfloat16)
    gate_sum = jnp.dot(normed, gate_weight, preferred_element_type=jnp.float32)
    up_sum = jnp.dot(normed, up_weight, preferred_element_type=jnp.float32)
    activated = (jax.nn.silu(gate_sum) * up_sum).astype(jnp.bfloat16)
    hidden_block = FSW // N_TENSOR

    def add_branch(index, total):
        offset = (index * hidden_block).astype(jnp.int32)
        columns = lax.dynamic_slice_in_dim(activated, offset, hidden_block, 1)
        weight_rows = lax.dynamic_slice_in_dim(down_weight, offset, hidden_block, 0)
        partial_sum = jnp.dot(columns, weight_rows, preferred_element_type=jnp.float32).astype(jnp.bfloat16)
        return total + lax.optimization_barrier(partial_sum).astype(jnp.float32)
    branch = lax.fori_loop(0, N_TENSOR, add_branch, jnp.zeros((TOKENS, DS), jnp.float32))
    predicted = student_wide + branch
    grad_rows = (token_weight.astype(jnp.float32)[:, None] * (predicted - projected.astype(jnp.float32)) / jnp.sqrt(jnp.float32(TOKENS))).astype(jnp.bfloat16)
    owner_list = owner_map[:, 0].reshape(owners, EPI_DEV)
    onehot = (owner_list[:, :, None] == jnp.arange(owners, dtype=jnp.int32)[None, None, :]).astype(jnp.int32)
    earlier = jnp.cumsum(onehot, axis=1) - onehot
    rank_list = lax.optimization_barrier(jnp.sum(earlier * onehot, axis=2))
    target = owner_list * CAP + rank_list
    wanted = jnp.arange(owners, dtype=jnp.int32)[:, None] * CAP + jnp.arange(CAP, dtype=jnp.int32)[None, :]
    matches = (target[None, :, None, :] == wanted[:, None, :, None]).astype(jnp.int32)
    found = lax.optimization_barrier(jnp.sum(matches, axis=3))
    chosen = lax.optimization_barrier(jnp.sum(matches * jnp.arange(EPI_DEV, dtype=jnp.int32)[None, None, None, :], axis=3))
    source_index = jnp.arange(owners, dtype=jnp.int32)[None, None, :, None]
    place_index = jnp.arange(EP_LEN, dtype=jnp.int32)[None, :, None, None]
    row_index = (source_index * EP_LEN + place_index) * EPI_DEV + chosen[:, None, :, :]
    row_index = jnp.where(found[:, None, :, :] > 0, row_index, TOKENS).astype(jnp.int32)
    row_index = row_index.reshape(owners, EP_LEN * owners * CAP)
    padded_out = jnp.concatenate([predicted.astype(jnp.bfloat16), jnp.zeros((1, DS), jnp.bfloat16)], axis=0)
    student_out = jnp.take(padded_out, row_index.reshape(-1), axis=0).reshape(owners, EP_LEN, RECV, DS)
    grad_padded = jnp.concatenate([grad_rows, jnp.zeros((1, DS), jnp.bfloat16)], axis=0)
    act_padded = jnp.concatenate([activated, jnp.zeros((1, FSW), jnp.bfloat16)], axis=0)

    def add_owner(index, total):
        chosen_rows = row_index[index]
        grad_part = jnp.take(grad_padded, chosen_rows, axis=0).astype(jnp.float32)
        act_part = jnp.take(act_padded, chosen_rows, axis=0).astype(jnp.float32)
        term = jnp.einsum('rc,rh->ch', grad_part, act_part)
        return total + lax.optimization_barrier(term.astype(jnp.bfloat16)).astype(jnp.float32)
    down_grad = lax.fori_loop(0, owners, add_owner, jnp.zeros((DS, FSW), jnp.float32))
    return (student_out, down_grad)
```

```python
import math

import jax
import jax.numpy as jnp
from jax import lax
from jax.sharding import Mesh
from jax.sharding import PartitionSpec as P

DT = 8192
EP_LEN = 16
TENSOR = ("tensor_0", "tensor_1")
OWNERS = ("group", "dp")
GROUP_DP_TENSOR = ("group", "dp", "tensor_0", "tensor_1")
EPSILON = 1e-06


def build_selector(owner_local, owners, capacity):
    owner = owner_local[:, 0]
    index = jnp.arange(owner.shape[0], dtype=jnp.int32)
    earlier = (owner[None, :] == owner[:, None]) & (index[None, :] < index[:, None])
    target = owner * capacity + jnp.sum(earlier.astype(jnp.int32), axis=1)
    slots = jnp.arange(owners * capacity, dtype=jnp.int32)
    return (target[None, :] == slots[:, None]).astype(jnp.bfloat16)


def local(
    teacher_hidden,
    teacher_gain,
    project_weight,
    student_hidden,
    student_gain,
    gate_weight,
    up_weight,
    down_weight,
    owner_map,
    token_ids,
    token_counts,
    id_weight,
):
    owners = lax.axis_size(OWNERS)
    episodes = token_counts.shape[0]
    capacity = max(2, 2 * episodes // owners)
    hidden = gate_weight.shape[1]
    position = lax.axis_index(TENSOR)
    tokens_all = EP_LEN * episodes * owners

    student = student_hidden.astype(jnp.float32)
    rescale = lax.rsqrt(jnp.mean(student * student, axis=1, keepdims=True) + EPSILON)
    normed = (student * rescale * student_gain[None, :]).astype(jnp.bfloat16)
    gathered = lax.all_gather(normed, TENSOR, axis=0, tiled=True)

    both = lax.all_gather(
        jnp.concatenate([gate_weight, up_weight], axis=1), OWNERS, axis=0, tiled=True
    )
    down = lax.all_gather(down_weight, OWNERS, axis=1, tiled=True)

    widened = teacher_hidden.astype(jnp.float32)
    squares = jnp.sum(widened * widened, axis=1)
    scaled = (widened * teacher_gain[None, :]).astype(jnp.bfloat16)
    totals = lax.psum_scatter(squares, TENSOR, scatter_dimension=0, tiled=True)
    inverse = lax.rsqrt(totals / DT + EPSILON)
    summed = lax.psum_scatter(
        jnp.dot(scaled, project_weight, preferred_element_type=jnp.float32).astype(jnp.bfloat16),
        TENSOR,
        scatter_dimension=0,
        tiled=True,
    ).astype(jnp.float32)
    projected = (summed * inverse[:, None]).astype(jnp.bfloat16).astype(jnp.float32)

    sums = jnp.dot(gathered, both, preferred_element_type=jnp.float32)
    activated = (jax.nn.silu(sums[:, :hidden]) * sums[:, hidden:]).astype(jnp.bfloat16)
    branch = jnp.dot(activated, down, preferred_element_type=jnp.float32).astype(jnp.bfloat16)
    branch_local = lax.psum_scatter(branch, TENSOR, scatter_dimension=0, tiled=True)
    predicted = student + branch_local.astype(jnp.float32)

    ids = jnp.arange(id_weight.shape[0], dtype=jnp.int32)
    looked = jnp.sum(jnp.where(token_ids[:, None] == ids[None, :], id_weight[None, :], 0.0), axis=1)
    weight = jnp.where(position < token_counts, looked, 0.0).astype(jnp.bfloat16)
    scale = 1.0 / math.sqrt(tokens_all)
    grad = (weight.astype(jnp.float32)[:, None] * (predicted - projected) * scale).astype(
        jnp.bfloat16
    )
    grad_all = lax.all_gather(grad, TENSOR, axis=0, tiled=True)
    down_grad = lax.psum_scatter(
        jnp.einsum("rc,rh->ch", grad_all, activated, preferred_element_type=jnp.float32).astype(
            jnp.bfloat16
        ),
        OWNERS,
        scatter_dimension=0,
        tiled=True,
    ).astype(jnp.float32)

    selector = build_selector(owner_map, owners, capacity)
    sent = jnp.dot(
        selector, predicted.astype(jnp.bfloat16), preferred_element_type=jnp.float32
    ).astype(jnp.bfloat16)
    student_out = lax.all_to_all(sent, OWNERS, 0, 0, tiled=True)
    return (student_out[None, None], down_grad)


def solution(mesh):
    split = Mesh(
        mesh.devices.reshape(mesh.shape["group"], mesh.shape["dp"], 4, 4),
        ("group", "dp", "tensor_0", "tensor_1"),
    )
    placed = (
        P(OWNERS, TENSOR),
        P(TENSOR),
        P(TENSOR, None),
        P(GROUP_DP_TENSOR, None),
        P(),
        P(OWNERS, TENSOR),
        P(OWNERS, TENSOR),
        P(TENSOR, OWNERS),
        P(OWNERS, None),
        P(GROUP_DP_TENSOR),
        P(OWNERS),
        P(),
    )
    return jax.shard_map(
        local,
        mesh=split,
        in_specs=placed,
        out_specs=(P(OWNERS, TENSOR, None, None), P(OWNERS, TENSOR)),
        check_vma=False,
    )
```

```python
import math

import jax
import jax.numpy as jnp
from jax import lax
from jax.sharding import Mesh
from jax.sharding import PartitionSpec as P

DT = 8192
EP_LEN = 16
AXES = {"group": 2, "x": 4, "core": 2, "z": 4, "y": 4}
OWNERS = ("group", "x", "core")
TENSOR = ("z", "y")
EPSILON = 1e-06
F32 = jnp.float32
BF16 = jnp.bfloat16


def shift(array, axis, by):
    size = AXES[axis]
    return lax.ppermute(array, axis, [(i, (i + by) % size) for i in range(size)])


def rolled(array, axis, name):
    doubled = jnp.concatenate([array, array], axis=axis)
    return lax.dynamic_slice_in_dim(doubled, lax.axis_index(name), array.shape[axis], axis)


def unrolled(array, axis, name):
    size = array.shape[axis]
    doubled = jnp.concatenate([array, array], axis=axis)
    return lax.dynamic_slice_in_dim(doubled, size - lax.axis_index(name), size, axis)


def relative_columns(rows):
    n = rows.shape[0]
    blocks = rows.reshape(n, 2, 4, 2, -1).transpose(1, 3, 2, 0, 4)
    blocks = rolled(rolled(rolled(blocks, 0, "group"), 1, "core"), 2, "x")
    return blocks.transpose(3, 0, 1, 2, 4).reshape(n, -1)


def absolute_columns(rows):
    n = rows.shape[0]
    blocks = rows.reshape(n, 2, 2, 4, -1).transpose(1, 2, 3, 0, 4)
    blocks = unrolled(unrolled(unrolled(blocks, 0, "group"), 1, "core"), 2, "x")
    return blocks.transpose(3, 0, 2, 1, 4).reshape(n, -1)


def gather_x(piece):
    half = piece.shape[0] // 2
    behind = shift(piece, "x", 1)
    ahead = shift(piece, "x", -1)
    top = shift(behind[:half], "x", 1)
    bottom = shift(ahead[half:], "x", -1)
    return jnp.concatenate([piece, ahead, top, bottom, behind], axis=0)


def weight_blocks(piece):
    own = gather_x(piece)
    return own, shift(own, "core", 1)


def gather_rows(rows):
    column = jnp.concatenate([rows, *(shift(rows, "z", -k) for k in (1, 2, 3))], axis=0)
    return jnp.concatenate([column, *(shift(column, "y", -k) for k in (1, 2, 3))], axis=0)


def scatter_axis(parts, axis):
    n = parts.shape[0] // 4
    arrived = [shift(parts[k * n : (k + 1) * n], axis, k) for k in (1, 2, 3)]
    total = parts[:n].astype(F32)
    for a in arrived:
        total = total + a.astype(F32)
    return total


def scatter_rows(parts):
    column = scatter_axis(parts, "y").astype(parts.dtype)
    return scatter_axis(column, "z")


def scatter_x(parts):
    n = parts.shape[0] // 4
    half = n // 2
    own, first, second, third = (parts[k * n : (k + 1) * n] for k in range(4))
    top = shift(second[:half], "x", 1)
    bottom = shift(second[half:], "x", -1)
    up = jnp.concatenate([first[:half] + top, first[half:]], axis=0)
    down = jnp.concatenate([third[:half], third[half:] + bottom], axis=0)
    from_behind = shift(up, "x", 1)
    from_ahead = shift(down, "x", -1)
    return own.astype(F32) + from_behind.astype(F32) + from_ahead.astype(F32)


def pick(onehot, rows):
    return jnp.dot(onehot.astype(BF16), rows, preferred_element_type=F32).astype(BF16)


def to_owners(rows, owner_local):
    owner = owner_local[:, 0]
    index = jnp.arange(owner.shape[0], dtype=jnp.int32)
    earlier = (owner[None, :] == owner[:, None]) & (index[None, :] < index[:, None])
    rank = jnp.sum(earlier.astype(jnp.int32), axis=1)
    g, x, c = (lax.axis_index(a) for a in OWNERS)
    to_c = (owner % 2 + c) % 2
    to_g = (owner // 8 + g) % 2
    to_x = (owner // 2 % 4 - x) % 4
    place = (to_g * 4 + to_x) * 2 + rank
    slots = jnp.arange(16, dtype=jnp.int32)[:, None]
    stay = pick((slots == place[None, :]) & (to_c[None, :] == 0), rows)
    leave = pick((slots == place[None, :]) & (to_c[None, :] == 1), rows)
    arrived = shift(leave, "core", 1)
    kept = jnp.concatenate([stay[:8], arrived[:8]], axis=0)
    sent = jnp.concatenate([stay[8:], arrived[8:]], axis=0)
    both = jnp.concatenate([kept, shift(sent, "group", 1)], axis=0)
    by_x = both.reshape(4, 4, 2, -1)
    groups = [by_x[:, k].reshape(8, -1) for k in range(4)]
    here = jnp.concatenate([groups[0], *(shift(groups[k], "x", k) for k in (1, 2, 3))], axis=0)
    source = jnp.arange(32, dtype=jnp.int32)
    k, sg, sc, r = source // 8, source // 4 % 2, source // 2 % 2, source % 2
    final = (((g + sg) % 2 * 4 + (x - k) % 4) * 2 + (c + sc) % 2) * 2 + r
    return pick(jnp.arange(32, dtype=jnp.int32)[:, None] == final[None, :], here)


def local(
    teacher_hidden,
    teacher_gain,
    project_weight,
    student_hidden,
    student_gain,
    gate_weight,
    up_weight,
    down_weight,
    owner_map,
    token_ids,
    token_counts,
    id_weight,
):
    episodes = token_counts.shape[0]
    hidden = gate_weight.shape[1]
    width = student_hidden.shape[1]
    block = width // 4
    position = lax.axis_index(TENSOR)
    tokens_all = EP_LEN * episodes * lax.axis_size(OWNERS)

    wide = student_hidden.astype(F32)
    rescale = lax.rsqrt(jnp.mean(wide * wide, axis=1, keepdims=True) + EPSILON)
    normed = (wide * rescale * student_gain[None, :]).astype(BF16)
    both_rows = relative_columns(jnp.concatenate([normed, student_hidden], axis=0))
    gathered = gather_rows(both_rows[:episodes])
    student = both_rows[episodes:].astype(F32)

    gate_up = jnp.concatenate([gate_weight, up_weight], axis=1)
    down = down_weight.T
    gate_up_far = shift(gate_up, "group", 1)
    down_far = shift(down, "group", 1)
    gate_up_blocks = [*weight_blocks(gate_up), *weight_blocks(gate_up_far)]
    down_blocks = [weight_blocks(down), weight_blocks(down_far)]

    teacher = teacher_hidden.reshape(4, 4, episodes, -1)
    teacher = rolled(rolled(teacher, 0, "z"), 1, "y").transpose(1, 0, 2, 3)
    widened = teacher.reshape(EP_LEN * episodes, -1).astype(F32)
    squares = jnp.sum(widened * widened, axis=1).reshape(EP_LEN, episodes)
    totals = scatter_axis(scatter_axis(squares, "y"), "z")[0]
    inverse = lax.rsqrt(totals / DT + EPSILON)
    scaled = (widened * teacher_gain[None, :]).astype(BF16)
    parts = jnp.dot(scaled, project_weight, preferred_element_type=F32).astype(BF16)
    projected = (scatter_rows(parts) * inverse[:, None]).astype(BF16)
    projected = relative_columns(projected).astype(F32)

    ids = jnp.arange(id_weight.shape[0], dtype=jnp.int32)
    looked = jnp.sum(jnp.where(token_ids[:, None] == ids[None, :], id_weight[None, :], 0.0), axis=1)
    weight = jnp.where(position < token_counts, looked, 0.0).astype(BF16).astype(F32)
    scale = 1.0 / math.sqrt(tokens_all)

    sums = None
    for k, w in enumerate(gate_up_blocks):
        part = jnp.dot(gathered[:, k * block : (k + 1) * block], w, preferred_element_type=F32)
        sums = part if sums is None else sums + part
    activated = (jax.nn.silu(sums[:, :hidden]) * sums[:, hidden:]).astype(BF16)

    predicted, reduced = [None, None], [None, None]
    for far in (1, 0):
        columns = slice(far * 2 * block, (far + 1) * 2 * block)
        branch = jnp.concatenate(
            [
                jnp.einsum("rh,ch->rc", activated, w, preferred_element_type=F32).astype(BF16)
                for w in down_blocks[far]
            ],
            axis=1,
        )
        predicted[far] = student[:, columns] + scatter_rows(branch)
        difference = predicted[far] - projected[:, columns]
        grad = gather_rows((weight[:, None] * difference * scale).astype(BF16))
        mine, other = (
            jnp.einsum("rc,rh->ch", grad[:, a : a + block], activated, preferred_element_type=F32)
            .astype(BF16)
            for a in (0, block)
        )
        reduced[far] = scatter_x(mine + shift(other, "core", 1))
    down_grad = reduced[0] + shift(reduced[1].astype(BF16), "group", 1).astype(F32)

    rows = jnp.concatenate([p.astype(BF16) for p in predicted], axis=1)
    student_out = to_owners(absolute_columns(rows), owner_map)
    return (student_out[None, None], down_grad)


def solution(mesh):
    split = Mesh(mesh.devices.reshape(*AXES.values()), tuple(AXES))
    placed = (
        P(OWNERS, TENSOR),
        P(TENSOR),
        P(TENSOR, None),
        P((*OWNERS, *TENSOR), None),
        P(),
        P(OWNERS, TENSOR),
        P(OWNERS, TENSOR),
        P(TENSOR, OWNERS),
        P(OWNERS, None),
        P((*OWNERS, *TENSOR)),
        P(OWNERS),
        P(),
    )
    return jax.shard_map(
        local,
        mesh=split,
        in_specs=placed,
        out_specs=(P(OWNERS, TENSOR, None, None), P(OWNERS, TENSOR)),
        check_vma=False,
    )
```

```python
import math

import jax
import jax.numpy as jnp
from jax import lax
from jax.experimental.layout import Layout, with_layout_constraint
from jax.sharding import Mesh
from jax.sharding import PartitionSpec as P

DT = 8192
EP_LEN = 16
AXES = {"group": 2, "x": 4, "core": 2, "z": 4, "y": 4}
OWNERS = ("group", "x", "core")
TENSOR = ("z", "y")
EPSILON = 1e-06
F32 = jnp.float32
BF16 = jnp.bfloat16


def shift(array, axis, by):
    size = AXES[axis]
    return lax.ppermute(array, axis, [(i, (i + by) % size) for i in range(size)])


def rolled(array, axis, name):
    doubled = jnp.concatenate([array, array], axis=axis)
    return lax.dynamic_slice_in_dim(doubled, lax.axis_index(name), array.shape[axis], axis)


def unrolled(array, axis, name):
    size = array.shape[axis]
    doubled = jnp.concatenate([array, array], axis=axis)
    return lax.dynamic_slice_in_dim(doubled, size - lax.axis_index(name), size, axis)


def crossed(array, axis, name):
    shape = array.shape
    pairs = array.reshape(*shape[:axis], 2, 2, *shape[axis + 1 :])
    index = lax.axis_index(name)
    for bit, at in ((index // 2, axis), (index % 2, axis + 1)):
        pairs = jnp.where(bit == 1, jnp.flip(pairs, at), pairs)
    return pairs.reshape(shape)


def exchange(array, axis, bits):
    return lax.ppermute(array, axis, [(i, i ^ bits) for i in range(AXES[axis])])


def relative_columns(rows):
    n = rows.shape[0]
    blocks = rows.reshape(n, 2, 4, 2, -1).transpose(1, 3, 2, 0, 4)
    blocks = rolled(rolled(rolled(blocks, 0, "group"), 1, "core"), 2, "x")
    return blocks.transpose(3, 0, 1, 2, 4).reshape(n, -1)


def absolute_columns(rows):
    n = rows.shape[0]
    blocks = rows.reshape(n, 2, 2, 4, -1).transpose(1, 2, 3, 0, 4)
    blocks = unrolled(unrolled(unrolled(blocks, 0, "group"), 1, "core"), 2, "x")
    return blocks.transpose(3, 0, 2, 1, 4).reshape(n, -1)


def after(array, *earlier):
    return lax.optimization_barrier((array, *earlier))[0]


def gather_ring(piece, axis):
    half = piece.shape[0] // 2
    behind = shift(piece, axis, 1)
    ahead = shift(piece, axis, -1)
    top = shift(behind[:half], axis, 1)
    bottom = shift(ahead[half:], axis, -1)
    whole = jnp.concatenate([piece, ahead, top, bottom, behind], axis=0)
    return whole, (ahead, behind), (top, bottom)


def weight_blocks(piece):
    own, first, last = gather_ring(piece, "x")
    other = with_layout_constraint(shift(own, "core", 1), Layout((0, 1)))
    return (own, other), first, last


def gather_z(rows):
    return jnp.concatenate([rows, *(exchange(rows, "z", k) for k in (1, 2, 3))], axis=0)


def gather_z_doubling(rows):
    pair = jnp.concatenate([rows, exchange(rows, "z", 1)], axis=0)
    return jnp.concatenate([pair, exchange(pair, "z", 2)], axis=0)


def gather_y(rows):
    return jnp.concatenate([rows, *(shift(rows, "y", -k) for k in (1, 2, 3))], axis=0)


def added(parts, arrived):
    total = parts.astype(F32)
    for a in arrived:
        total = total + a.astype(F32)
    return total


def scatter_y(parts):
    n = parts.shape[0] // 4
    return added(parts[:n], [shift(parts[k * n : (k + 1) * n], "y", k) for k in (1, 2, 3)])


def scatter_z(parts):
    n = parts.shape[0] // 4
    return added(parts[:n], [exchange(parts[k * n : (k + 1) * n], "z", k) for k in (1, 2, 3)])


def scatter_z_halving(parts):
    n = parts.shape[0] // 4
    pair = added(parts[: 2 * n], [exchange(parts[2 * n :], "z", 2)])
    return added(pair[:n], [exchange(pair[n:].astype(BF16), "z", 1)])


def scatter_ring(parts, axis):
    n = parts.shape[0] // 4
    half = n // 2
    own, first, second, third = (parts[k * n : (k + 1) * n] for k in range(4))
    top = shift(second[:half], axis, 1)
    bottom = shift(second[half:], axis, -1)
    up = jnp.concatenate([first[:half] + top, first[half:]], axis=0)
    down = jnp.concatenate([third[:half], third[half:] + bottom], axis=0)
    return added(own, [shift(up, axis, 1), shift(down, axis, -1)])


def two_parts(values):
    high = lax.reduce_precision(values, 8, 7)
    both = jnp.concatenate([high, values - high], axis=1).astype(BF16)
    return jnp.pad(both, ((0, 0), (0, 128 - both.shape[1])))


def pick(onehot, rows):
    return jnp.dot(onehot.astype(BF16), rows, preferred_element_type=F32).astype(BF16)


def to_owners(rows, owner_local, gate):
    owner = owner_local[:, 0]
    index = jnp.arange(owner.shape[0], dtype=jnp.int32)
    earlier = (owner[None, :] == owner[:, None]) & (index[None, :] < index[:, None])
    rank = jnp.sum(earlier.astype(jnp.int32), axis=1)
    g, x, c = (lax.axis_index(a) for a in OWNERS)
    to_c = (owner % 2 + c) % 2
    to_g = (owner // 8 + g) % 2
    to_x = (owner // 2 % 4 - x) % 4
    place = (to_g * 4 + to_x) * 2 + rank
    slots = jnp.arange(16, dtype=jnp.int32)[:, None]
    stay = pick((slots == place[None, :]) & (to_c[None, :] == 0), rows)
    leave = pick((slots == place[None, :]) & (to_c[None, :] == 1), rows)
    arrived = shift(leave, "core", 1)
    kept = jnp.concatenate([stay[:8], arrived[:8]], axis=0)
    sent = after(jnp.concatenate([stay[8:], arrived[8:]], axis=0), gate)
    both = jnp.concatenate([kept, shift(sent, "group", 1)], axis=0)
    by_x = both.reshape(4, 4, 2, -1)
    groups = [by_x[:, k].reshape(8, -1) for k in range(4)]
    here = jnp.concatenate([groups[0], *(shift(groups[k], "x", k) for k in (1, 2, 3))], axis=0)
    source = jnp.arange(32, dtype=jnp.int32)
    k, sg, sc, r = source // 8, source // 4 % 2, source // 2 % 2, source % 2
    final = (((g + sg) % 2 * 4 + (x - k) % 4) * 2 + (c + sc) % 2) * 2 + r
    return pick(jnp.arange(32, dtype=jnp.int32)[:, None] == final[None, :], here)


def local(
    teacher_hidden,
    teacher_gain,
    project_weight,
    student_hidden,
    student_gain,
    gate_weight,
    up_weight,
    down_weight,
    owner_map,
    token_ids,
    token_counts,
    id_weight,
):
    episodes = token_counts.shape[0]
    hidden = gate_weight.shape[1]
    width = student_hidden.shape[1]
    block = width // 4
    position = lax.axis_index(TENSOR)
    tokens_all = EP_LEN * episodes * lax.axis_size(OWNERS)

    down = down_weight.T
    gate_up = jnp.concatenate([gate_weight, up_weight], axis=1)
    near = jnp.concatenate([down, gate_weight, up_weight], axis=1)
    near_blocks, near_first, near_last = weight_blocks(near)
    gate_up_far = shift(gate_up, "group", 1)
    down_far = shift(after(down, gate_up_far), "group", 1)
    far_blocks, far_first, _ = weight_blocks(after(gate_up_far, *near_last))
    down_far_blocks, _, _ = weight_blocks(after(down_far, *far_first))

    student_hidden, teacher_hidden = after(student_hidden, near), after(teacher_hidden, near)
    wide = student_hidden.astype(F32)
    rescale = lax.rsqrt(jnp.mean(wide * wide, axis=1, keepdims=True) + EPSILON)
    normed = (wide * rescale * student_gain[None, :]).astype(BF16)
    both_rows = relative_columns(jnp.concatenate([normed, student_hidden], axis=0))
    student = both_rows[episodes:].astype(F32)
    widened = teacher_hidden.astype(F32)
    squares = jnp.sum(widened * widened, axis=1).reshape(EP_LEN, episodes).T
    column = gather_z_doubling(jnp.concatenate([both_rows[:episodes], two_parts(squares)], axis=1))
    gathered, _, gathered_last = gather_ring(after(column, *near_first), "y")
    totals = jnp.sum(gathered[:, width:].reshape(EP_LEN, episodes, -1).astype(F32), axis=0)
    totals = totals[:, :EP_LEN] + totals[:, EP_LEN : 2 * EP_LEN]
    totals = jnp.sum(jnp.where(jnp.arange(EP_LEN)[None, :] == position, totals, 0.0), axis=1)
    inverse = lax.rsqrt(totals / DT + EPSILON)

    teacher = after(teacher_hidden, *near_first).reshape(4, 4, episodes, -1)
    teacher = rolled(crossed(teacher, 0, "z"), 1, "y").transpose(1, 0, 2, 3)
    widened = teacher.reshape(EP_LEN * episodes, -1).astype(F32)
    scaled = (widened * teacher_gain[None, :]).astype(BF16)
    parts = jnp.dot(scaled, project_weight, preferred_element_type=F32).astype(BF16)
    total = scatter_z_halving(scatter_ring(after(parts, *gathered_last), "y").astype(BF16))
    projected = (total * inverse[:, None]).astype(BF16)
    projected = relative_columns(projected).astype(F32)

    ids = jnp.arange(id_weight.shape[0], dtype=jnp.int32)
    looked = jnp.sum(jnp.where(token_ids[:, None] == ids[None, :], id_weight[None, :], 0.0), axis=1)
    weight = jnp.where(position < token_counts, looked, 0.0).astype(BF16).astype(F32)
    scale = 1.0 / math.sqrt(tokens_all)

    def times(k, w):
        return jnp.dot(gathered[:, k * block : (k + 1) * block], w, preferred_element_type=F32)

    near_sums = times(0, near_blocks[0]) + times(1, near_blocks[1])
    sums = near_sums[:, hidden:] + times(2, far_blocks[0]) + times(3, far_blocks[1])
    activated = (jax.nn.silu(sums[:, :hidden]) * sums[:, hidden:]).astype(BF16)

    down_blocks = [[w[:, :hidden] for w in near_blocks], down_far_blocks]
    predicted, reduced, grads = [None, None], [None, None], [None, None]
    for far in (1, 0):
        columns = slice(far * 2 * block, (far + 1) * 2 * block)
        branch = jnp.concatenate(
            [
                jnp.einsum("rh,ch->rc", activated, w, preferred_element_type=F32).astype(BF16)
                for w in down_blocks[far]
            ],
            axis=1,
        )
        predicted[far] = student[:, columns] + scatter_z(scatter_y(branch).astype(BF16))
        difference = predicted[far] - projected[:, columns]
        grad = (weight[:, None] * difference * scale).astype(BF16)
        grads[far] = gather_y(gather_z(grad))
        mine, other = (
            jnp.einsum(
                "rc,rh->ch", grads[far][:, a : a + block], activated, preferred_element_type=F32
            ).astype(BF16)
            for a in (0, block)
        )
        reduced[far] = scatter_ring(mine + shift(other, "core", 1), "x")
    down_grad = reduced[0] + shift(reduced[1].astype(BF16), "group", 1).astype(F32)

    rows = jnp.concatenate([p.astype(BF16) for p in predicted], axis=1)
    student_out = to_owners(absolute_columns(rows), owner_map, grads[1])
    return (student_out[None, None], down_grad)


def solution(mesh):
    split = Mesh(mesh.devices.reshape(*AXES.values()), tuple(AXES))
    placed = (
        P(OWNERS, TENSOR),
        P(TENSOR),
        P(TENSOR, None),
        P((*OWNERS, *TENSOR), None),
        P(),
        P(OWNERS, TENSOR),
        P(OWNERS, TENSOR),
        P(TENSOR, OWNERS),
        P(OWNERS, None),
        P((*OWNERS, *TENSOR)),
        P(OWNERS),
        P(),
    )
    return jax.shard_map(
        local,
        mesh=split,
        in_specs=placed,
        out_specs=(P(OWNERS, TENSOR, None, None), P(OWNERS, TENSOR)),
        check_vma=False,
    )
```

```python
import math

import jax
import jax.numpy as jnp
from jax import lax
from jax.experimental import pallas as pl
from jax.experimental.pallas import tpu as pltpu
from jax.sharding import Mesh
from jax.sharding import PartitionSpec as P

DT = 8192
EP_LEN = 16
AXES = {"group": 2, "x": 4, "core": 2, "z": 4, "y": 4}
OWNERS = ("group", "x", "core")
TENSOR = ("z", "y")
EPSILON = 1e-06
F32 = jnp.float32
BF16 = jnp.bfloat16


def shift(array, axis, by):
    size = AXES[axis]
    return lax.ppermute(array, axis, [(i, (i + by) % size) for i in range(size)])


def rolled(array, axis, name):
    doubled = jnp.concatenate([array, array], axis=axis)
    return lax.dynamic_slice_in_dim(doubled, lax.axis_index(name), array.shape[axis], axis)


def unrolled(array, axis, name):
    size = array.shape[axis]
    doubled = jnp.concatenate([array, array], axis=axis)
    return lax.dynamic_slice_in_dim(doubled, size - lax.axis_index(name), size, axis)


def crossed(array, axis, name):
    shape = array.shape
    pairs = array.reshape(*shape[:axis], 2, 2, *shape[axis + 1 :])
    index = lax.axis_index(name)
    for bit, at in ((index // 2, axis), (index % 2, axis + 1)):
        pairs = jnp.where(bit == 1, jnp.flip(pairs, at), pairs)
    return pairs.reshape(shape)


def exchange(array, axis, bits):
    return lax.ppermute(array, axis, [(i, i ^ bits) for i in range(AXES[axis])])


def relative_columns(rows):
    n = rows.shape[0]
    blocks = rows.reshape(n, 2, 4, 2, -1).transpose(1, 3, 2, 0, 4)
    blocks = rolled(rolled(rolled(blocks, 0, "group"), 1, "core"), 2, "x")
    return blocks.transpose(3, 0, 1, 2, 4).reshape(n, -1)


def absolute_columns(rows):
    n = rows.shape[0]
    blocks = rows.reshape(n, 2, 2, 4, -1).transpose(1, 2, 3, 0, 4)
    blocks = unrolled(unrolled(unrolled(blocks, 0, "group"), 1, "core"), 2, "x")
    return blocks.transpose(3, 0, 2, 1, 4).reshape(n, -1)


def after(array, *earlier):
    return lax.optimization_barrier((array, *earlier))[0]


def ring_pieces(piece, axis):
    half = piece.shape[0] // 2
    behind = shift(piece, axis, 1)
    ahead = shift(piece, axis, -1)
    top = shift(behind[:half], axis, 1)
    bottom = shift(ahead[half:], axis, -1)
    return [piece, ahead, top, bottom, behind]


def swapped(pieces):
    return [shift(p, "core", 1) for p in pieces]


def joined_product(rows, at, pieces, near=None):
    tokens, width = rows.shape[0], sum(p.shape[0] for p in pieces)
    columns = pieces[0].shape[1]
    starts = [sum(p.shape[0] for p in pieces[:k]) for k in range(len(pieces))]
    middle = len(pieces) // 2

    def kernel(rows_ref, *refs):
        piece_refs, rest = refs[: len(pieces)], refs[len(pieces) :]
        out_ref, whole, sems = rest[-3:]
        copies = [
            pltpu.make_async_copy(p, whole.at[pl.ds(start, p.shape[0]), :], sems.at[k])
            for k, (p, start) in enumerate(zip(piece_refs, starts))
        ]
        for c in copies:
            c.start()
        total = None if near is None else rest[0][...]
        for group in (range(middle), range(middle, len(pieces))):
            for k in group:
                copies[k].wait()
            low = starts[group[0]]
            span = slice(low, low + width // 2)
            part = jnp.dot(rows_ref[:, span], whole[span, :], preferred_element_type=F32)
            total = part if total is None else total + part
        if near is None:
            out_ref[...] = total[:, columns - out_ref.shape[1] :]
        else:
            gate, up = total[:, : columns // 2], total[:, columns // 2 :]
            out_ref[...] = (gate / (1.0 + jnp.exp(-gate)) * up).astype(BF16)

    out = (
        jax.ShapeDtypeStruct((tokens, 2 * columns // 3), F32)
        if near is None
        else jax.ShapeDtypeStruct((tokens, columns // 2), BF16)
    )
    return pl.pallas_call(
        kernel,
        grid=(1,),
        in_specs=[
            pl.BlockSpec((tokens, width), lambda i: (0, at)),
            *(pl.BlockSpec(memory_space=pl.ANY) for _ in pieces),
            *([] if near is None else [pl.BlockSpec(near.shape, lambda i: (0, 0))]),
        ],
        out_specs=pl.BlockSpec(out.shape, lambda i: (0, 0)),
        out_shape=out,
        scratch_shapes=[
            pltpu.VMEM((width, columns), BF16),
            pltpu.SemaphoreType.DMA((len(pieces),)),
        ],
        compiler_params=pltpu.CompilerParams(vmem_limit_bytes=40 * 2**20),
    )(rows, *pieces, *([] if near is None else [near]))


def gather_z(rows):
    return jnp.concatenate([rows, *(exchange(rows, "z", k) for k in (1, 2, 3))], axis=0)


def gather_z_doubling(rows):
    pair = jnp.concatenate([rows, exchange(rows, "z", 1)], axis=0)
    return jnp.concatenate([pair, exchange(pair, "z", 2)], axis=0)


def gather_y(rows):
    return jnp.concatenate([rows, *(shift(rows, "y", -k) for k in (1, 2, 3))], axis=0)


def added(parts, arrived):
    total = parts.astype(F32)
    for a in arrived:
        total = total + a.astype(F32)
    return total


def scatter_y(parts):
    n = parts.shape[0] // 4
    return added(parts[:n], [shift(parts[k * n : (k + 1) * n], "y", k) for k in (1, 2, 3)])


def scatter_z(parts):
    n = parts.shape[0] // 4
    return added(parts[:n], [exchange(parts[k * n : (k + 1) * n], "z", k) for k in (1, 2, 3)])


def scatter_z_halving(parts):
    n = parts.shape[0] // 4
    pair = added(parts[: 2 * n], [exchange(parts[2 * n :], "z", 2)])
    return added(pair[:n], [exchange(pair[n:].astype(BF16), "z", 1)])


def scatter_ring(parts, axis, *gates):
    n = parts.shape[0] // 4
    half = n // 2
    own, first, second, third = (parts[k * n : (k + 1) * n] for k in range(4))
    top = shift(second[:half], axis, 1)
    bottom = shift(second[half:], axis, -1)
    up = jnp.concatenate([first[:half] + top, first[half:]], axis=0)
    down = jnp.concatenate([third[:half], third[half:] + bottom], axis=0)
    up, down = after(up, *gates), after(down, *gates)
    return added(own, [shift(up, axis, 1), shift(down, axis, -1)])


def two_parts(values):
    high = lax.reduce_precision(values, 8, 7)
    both = jnp.concatenate([high, values - high], axis=1).astype(BF16)
    return jnp.pad(both, ((0, 0), (0, 128 - both.shape[1])))


def pick(onehot, rows):
    return jnp.dot(onehot.astype(BF16), rows, preferred_element_type=F32).astype(BF16)


def to_owners(rows, owner_local, gate):
    owner = owner_local[:, 0]
    index = jnp.arange(owner.shape[0], dtype=jnp.int32)
    earlier = (owner[None, :] == owner[:, None]) & (index[None, :] < index[:, None])
    rank = jnp.sum(earlier.astype(jnp.int32), axis=1)
    g, x, c = (lax.axis_index(a) for a in OWNERS)
    to_c = (owner % 2 + c) % 2
    to_g = (owner // 8 + g) % 2
    to_x = (owner // 2 % 4 - x) % 4
    place = (to_g * 4 + to_x) * 2 + rank
    slots = jnp.arange(16, dtype=jnp.int32)[:, None]
    stay = pick((slots == place[None, :]) & (to_c[None, :] == 0), rows)
    leave = pick((slots == place[None, :]) & (to_c[None, :] == 1), rows)
    arrived = shift(leave, "core", 1)
    kept = jnp.concatenate([stay[:8], arrived[:8]], axis=0)
    sent = after(jnp.concatenate([stay[8:], arrived[8:]], axis=0), gate)
    both = jnp.concatenate([kept, shift(sent, "group", 1)], axis=0)
    by_x = both.reshape(4, 4, 2, -1)
    groups = [by_x[:, k].reshape(8, -1) for k in range(4)]
    here = jnp.concatenate([groups[0], *(shift(groups[k], "x", k) for k in (1, 2, 3))], axis=0)
    source = jnp.arange(32, dtype=jnp.int32)
    k, sg, sc, r = source // 8, source // 4 % 2, source // 2 % 2, source % 2
    final = (((g + sg) % 2 * 4 + (x - k) % 4) * 2 + (c + sc) % 2) * 2 + r
    return pick(jnp.arange(32, dtype=jnp.int32)[:, None] == final[None, :], here)


def local(
    teacher_hidden,
    teacher_gain,
    project_weight,
    student_hidden,
    student_gain,
    gate_weight,
    up_weight,
    down_weight,
    owner_map,
    token_ids,
    token_counts,
    id_weight,
):
    episodes = token_counts.shape[0]
    hidden = gate_weight.shape[1]
    width = student_hidden.shape[1]
    block = width // 4
    position = lax.axis_index(TENSOR)
    tokens_all = EP_LEN * episodes * lax.axis_size(OWNERS)

    down = down_weight.T
    gate_up = jnp.concatenate([gate_weight, up_weight], axis=1)
    near = jnp.concatenate([down, gate_up], axis=1)
    near_own = ring_pieces(near, "x")
    gate_up_far = shift(gate_up, "group", 1)
    near_other = swapped(near_own)
    far_own = ring_pieces(after(gate_up_far, *near_own[2:4]), "x")
    far_other = swapped(far_own)

    student_hidden, teacher_hidden = after(student_hidden, near), after(teacher_hidden, near)
    wide = student_hidden.astype(F32)
    rescale = lax.rsqrt(jnp.mean(wide * wide, axis=1, keepdims=True) + EPSILON)
    normed = (wide * rescale * student_gain[None, :]).astype(BF16)
    both_rows = relative_columns(jnp.concatenate([normed, student_hidden], axis=0))
    student = both_rows[episodes:].astype(F32)
    widened = teacher_hidden.astype(F32)
    squares = jnp.sum(widened * widened, axis=1).reshape(EP_LEN, episodes).T
    column = jnp.concatenate([both_rows[:episodes], two_parts(squares)], axis=1)
    column = gather_z_doubling(after(column, gate_up_far, *near_own[2:4]))
    down_far = shift(after(down, column), "group", 1)
    down_far_own = jnp.concatenate(ring_pieces(after(down_far, far_own[1], far_own[4]), "x"), axis=0)
    down_far_other = shift(down_far_own, "core", 1)
    gathered_pieces = ring_pieces(column, "y")
    gathered = jnp.concatenate(gathered_pieces, axis=0)
    totals = jnp.sum(gathered[:, width:].reshape(EP_LEN, episodes, -1).astype(F32), axis=0)
    totals = totals[:, :EP_LEN] + totals[:, EP_LEN : 2 * EP_LEN]
    totals = jnp.sum(jnp.where(jnp.arange(EP_LEN)[None, :] == position, totals, 0.0), axis=1)
    inverse = lax.rsqrt(totals / DT + EPSILON)

    teacher = teacher_hidden.reshape(4, 4, episodes, -1)
    teacher = rolled(crossed(teacher, 0, "z"), 1, "y").transpose(1, 0, 2, 3)
    widened = teacher.reshape(EP_LEN * episodes, -1).astype(F32)
    scaled = (widened * teacher_gain[None, :]).astype(BF16)
    parts = jnp.dot(scaled, project_weight, preferred_element_type=F32).astype(BF16)
    total = scatter_ring(parts, "y", gate_up_far, *near_own[2:4]).astype(BF16)
    total = scatter_z_halving(after(total, gathered))
    projected = (total * inverse[:, None]).astype(BF16)
    projected = relative_columns(projected).astype(F32)

    ids = jnp.arange(id_weight.shape[0], dtype=jnp.int32)
    looked = jnp.sum(jnp.where(token_ids[:, None] == ids[None, :], id_weight[None, :], 0.0), axis=1)
    weight = jnp.where(position < token_counts, looked, 0.0).astype(BF16).astype(F32)
    scale = 1.0 / math.sqrt(tokens_all)

    near_sums = joined_product(gathered, 0, near_own + near_other)
    activated = joined_product(gathered, 1, far_own + far_other, after(near_sums, projected))

    down_blocks = [
        [jnp.concatenate([p[:, :hidden] for p in pieces], axis=0) for pieces in (near_own, near_other)],
        [down_far_own, down_far_other],
    ]

    def branch_half(far, activated):
        return jnp.concatenate(
            [
                jnp.einsum("rh,ch->rc", activated, w, preferred_element_type=F32).astype(BF16)
                for w in down_blocks[far]
            ],
            axis=1,
        )

    def gradient_half(far, branch_rows):
        columns = slice(far * 2 * block, (far + 1) * 2 * block)
        predicted = student[:, columns] + scatter_z(branch_rows)
        difference = predicted - projected[:, columns]
        return predicted, gather_z((weight[:, None] * difference * scale).astype(BF16))

    def owners_half(grad):
        mine, other = (
            jnp.einsum(
                "rc,rh->ch", grad[:, a : a + block], activated, preferred_element_type=F32
            ).astype(BF16)
            for a in (0, block)
        )
        return scatter_ring(mine + shift(other, "core", 1), "x")

    far_branch = branch_half(1, activated)
    near_branch = branch_half(0, after(activated, far_branch))
    far_rows = scatter_y(far_branch).astype(BF16)
    near_rows = scatter_y(after(near_branch, far_rows)).astype(BF16)
    far_predicted, far_column = gradient_half(1, far_rows)
    near_predicted, near_column = gradient_half(0, near_rows)
    far_grad = gather_y(far_column)
    near_grad = gather_y(after(near_column, far_grad))
    far_reduced = owners_half(far_grad)
    near_reduced = owners_half(near_grad)
    down_grad = near_reduced + shift(far_reduced.astype(BF16), "group", 1).astype(F32)

    predicted = [near_predicted, far_predicted]
    rows = jnp.concatenate([p.astype(BF16) for p in predicted], axis=1)
    student_out = to_owners(absolute_columns(rows), owner_map, far_grad)
    return (student_out[None, None], down_grad)


def solution(mesh):
    split = Mesh(mesh.devices.reshape(*AXES.values()), tuple(AXES))
    placed = (
        P(OWNERS, TENSOR),
        P(TENSOR),
        P(TENSOR, None),
        P((*OWNERS, *TENSOR), None),
        P(),
        P(OWNERS, TENSOR),
        P(OWNERS, TENSOR),
        P(TENSOR, OWNERS),
        P(OWNERS, None),
        P((*OWNERS, *TENSOR)),
        P(OWNERS),
        P(),
    )
    return jax.shard_map(
        local,
        mesh=split,
        in_specs=placed,
        out_specs=(P(OWNERS, TENSOR, None, None), P(OWNERS, TENSOR)),
        check_vma=False,
    )
```

```python
import math

import jax
import jax.numpy as jnp
from jax import lax
from jax.experimental import pallas as pl
from jax.experimental.pallas import tpu as pltpu
from jax.sharding import Mesh
from jax.sharding import PartitionSpec as P

DT = 8192
EP_LEN = 16
AXES = {"group": 2, "x": 4, "core": 2, "z": 4, "y": 4}
OWNERS = ("group", "x", "core")
TENSOR = ("z", "y")
EPSILON = 1e-06
F32 = jnp.float32
BF16 = jnp.bfloat16


def shift(array, axis, by):
    size = AXES[axis]
    return lax.ppermute(array, axis, [(i, (i + by) % size) for i in range(size)])


def rolled(array, axis, name):
    doubled = jnp.concatenate([array, array], axis=axis)
    return lax.dynamic_slice_in_dim(doubled, lax.axis_index(name), array.shape[axis], axis)


def unrolled(array, axis, name):
    size = array.shape[axis]
    doubled = jnp.concatenate([array, array], axis=axis)
    return lax.dynamic_slice_in_dim(doubled, size - lax.axis_index(name), size, axis)


def crossed(array, axis, name):
    shape = array.shape
    pairs = array.reshape(*shape[:axis], 2, 2, *shape[axis + 1 :])
    index = lax.axis_index(name)
    for bit, at in ((index // 2, axis), (index % 2, axis + 1)):
        pairs = jnp.where(bit == 1, jnp.flip(pairs, at), pairs)
    return pairs.reshape(shape)


def exchange(array, axis, bits):
    return lax.ppermute(array, axis, [(i, i ^ bits) for i in range(AXES[axis])])


def relative_columns(rows):
    n = rows.shape[0]
    blocks = rows.reshape(n, 2, 4, 2, -1).transpose(1, 3, 2, 0, 4)
    blocks = rolled(rolled(rolled(blocks, 0, "group"), 1, "core"), 2, "x")
    return blocks.transpose(3, 0, 1, 2, 4).reshape(n, -1)


def absolute_columns(rows):
    n = rows.shape[0]
    blocks = rows.reshape(n, 2, 2, 4, -1).transpose(1, 2, 3, 0, 4)
    blocks = unrolled(unrolled(unrolled(blocks, 0, "group"), 1, "core"), 2, "x")
    return blocks.transpose(3, 0, 2, 1, 4).reshape(n, -1)


def after(array, *earlier):
    return lax.optimization_barrier((array, *earlier))[0]


def ring_pieces(piece, axis, *gates):
    half = (piece.shape[0] + 31) // 32 * 16
    behind = shift(piece, axis, 1)
    ahead = shift(piece, axis, -1)
    top = shift(after(behind[:half], *gates), axis, 1)
    bottom = shift(after(ahead[half:], *gates), axis, -1)
    return [piece, ahead, top, bottom, behind]


def swapped(pieces):
    return [shift(p, "core", 1) for p in pieces]


def ring_starts(pieces, block, low):
    return [low, low + block, low + 2 * block, low + 2 * block + pieces[2].shape[0], low + 3 * block]


def joined_product(rows, pieces, starts, skip):
    tokens, width, columns = rows.shape[0], sum(p.shape[0] for p in pieces), pieces[0].shape[1]
    count = len(pieces)

    def kernel(rows_ref, *refs):
        out_ref, whole, sems = refs[count:]
        copies = [
            pltpu.make_async_copy(refs[k], whole.at[pl.ds(starts[k], pieces[k].shape[0]), :], sems.at[k])
            for k in range(count)
        ]
        for c in copies:
            c.start()
        for c in copies:
            c.wait()
        total = jnp.dot(rows_ref[...], whole[...], preferred_element_type=F32)
        out_ref[...] = total[:, skip:]

    out = jax.ShapeDtypeStruct((tokens, columns - skip), F32)
    return pl.pallas_call(
        kernel,
        grid=(1,),
        in_specs=[
            pl.BlockSpec((tokens, width), lambda i: (0, 0)),
            *(pl.BlockSpec(memory_space=pltpu.HBM) for _ in pieces),
        ],
        out_specs=pl.BlockSpec(out.shape, lambda i: (0, 0)),
        out_shape=out,
        scratch_shapes=[pltpu.VMEM((width, columns), BF16), pltpu.SemaphoreType.DMA((count,))],
        compiler_params=pltpu.CompilerParams(vmem_limit_bytes=40 * 2**20),
    )(rows, *pieces)


def feed_forward(rows, near_sums, far, far_starts, near, near_starts, hidden):
    tokens, columns = rows.shape[0], far[0].shape[1]
    width = sum(p.shape[0] for p in far)
    lanes = -(-hidden // 128) * 128
    share = tokens // 4

    def kernel(rows_ref, near_sums_ref, *refs):
        far_refs, near_refs = refs[: len(far)], refs[len(far) : len(far) + len(near)]
        rest = refs[len(far) + len(near) :]
        activated_ref, far_outs, near_outs = rest[0], rest[1:5], rest[5:9]
        whole, near_down, padded, far_sems, near_sems = rest[9:]
        far_copies = [
            pltpu.make_async_copy(ref, whole.at[pl.ds(low, ref.shape[0]), :], far_sems.at[k])
            for k, (ref, low) in enumerate(zip(far_refs, far_starts))
        ]
        near_copies = [
            pltpu.make_async_copy(
                ref.at[:, pl.ds(0, lanes)], near_down.at[pl.ds(low, ref.shape[0]), :], near_sems.at[k]
            )
            for k, (ref, low) in enumerate(zip(near_refs, near_starts))
        ]
        for c in far_copies + near_copies:
            c.start()
        padded[...] = jnp.zeros_like(padded)
        for c in far_copies:
            c.wait()
        total = jnp.dot(rows_ref[...], whole[...], preferred_element_type=F32)[:, hidden:]
        total = total + near_sums_ref[...]
        gate, up = total[:, :hidden], total[:, hidden:]
        activated = (gate / (1.0 + jnp.exp(-gate)) * up).astype(BF16)
        activated_ref[...] = activated
        padded[:, :hidden] = activated
        for c in near_copies:
            c.wait()
        for down, outs in ((whole[:, :lanes], far_outs), (near_down[...], near_outs)):
            branch = lax.dot_general(
                padded[...], down, (((1,), (1,)), ((), ())), preferred_element_type=F32
            ).astype(BF16)
            for k, out in enumerate(outs):
                out[...] = branch[k * share : (k + 1) * share]

    block = jax.ShapeDtypeStruct((share, width), BF16)
    outs = [jax.ShapeDtypeStruct((tokens, hidden), BF16), *[block] * 8]
    activated, *blocks = pl.pallas_call(
        kernel,
        grid=(1,),
        in_specs=[
            pl.BlockSpec((tokens, width), lambda i: (0, 1)),
            pl.BlockSpec(near_sums.shape, lambda i: (0, 0)),
            *(pl.BlockSpec(memory_space=pltpu.HBM) for _ in far + near),
        ],
        out_specs=[pl.BlockSpec(o.shape, lambda i: (0, 0)) for o in outs],
        out_shape=outs,
        scratch_shapes=[
            pltpu.VMEM((width, columns), BF16),
            pltpu.VMEM((width, lanes), BF16),
            pltpu.VMEM((tokens, lanes), BF16),
            pltpu.SemaphoreType.DMA((len(far),)),
            pltpu.SemaphoreType.DMA((len(near),)),
        ],
        compiler_params=pltpu.CompilerParams(vmem_limit_bytes=40 * 2**20),
    )(rows, near_sums, *far, *near)
    return activated, blocks[:4], blocks[4:]


def gather_z(rows):
    return jnp.concatenate([rows, *(exchange(rows, "z", k) for k in (1, 2, 3))], axis=0)


def gather_z_doubling(rows):
    pair = jnp.concatenate([rows, exchange(rows, "z", 1)], axis=0)
    return jnp.concatenate([pair, exchange(pair, "z", 2)], axis=0)


def gather_y(rows):
    return jnp.concatenate([rows, *(shift(rows, "y", -k) for k in (1, 2, 3))], axis=0)


def added(parts, arrived):
    total = parts.astype(F32)
    for a in arrived:
        total = total + a.astype(F32)
    return total


def scatter_y(blocks):
    return added(blocks[0], [shift(blocks[k], "y", k) for k in (1, 2, 3)])


def scatter_z(parts):
    n = parts.shape[0] // 4
    return added(parts[:n], [exchange(parts[k * n : (k + 1) * n], "z", k) for k in (1, 2, 3)])


def scatter_z_halving(parts, *gates):
    n = parts.shape[0] // 4
    pair = added(parts[: 2 * n], [exchange(parts[2 * n :], "z", 2)])
    return added(pair[:n], [exchange(after(pair[n:].astype(BF16), *gates), "z", 1)])


def scatter_ring(own, first, top, bottom, third, axis, *gates):
    half = top.shape[0]
    top, bottom = shift(top, axis, 1), shift(bottom, axis, -1)
    up = jnp.concatenate([first[:half] + top, first[half:]], axis=0)
    down = jnp.concatenate([third[:half], third[half:] + bottom], axis=0)
    up, down = after(up, *gates), after(down, *gates)
    return added(own, [shift(up, axis, 1), shift(down, axis, -1)])


def two_parts(values):
    high = lax.reduce_precision(values, 8, 7)
    both = jnp.concatenate([high, values - high], axis=1).astype(BF16)
    return jnp.pad(both, ((0, 0), (0, 128 - both.shape[1])))


def pick(onehot, rows):
    return jnp.dot(onehot.astype(BF16), rows, preferred_element_type=F32).astype(BF16)


def to_owners(rows, owner_local, gate):
    owner = owner_local[:, 0]
    index = jnp.arange(owner.shape[0], dtype=jnp.int32)
    earlier = (owner[None, :] == owner[:, None]) & (index[None, :] < index[:, None])
    rank = jnp.sum(earlier.astype(jnp.int32), axis=1)
    g, x, c = (lax.axis_index(a) for a in OWNERS)
    to_c = (owner % 2 + c) % 2
    to_g = (owner // 8 + g) % 2
    to_x = (owner // 2 % 4 - x) % 4
    place = (to_g * 4 + to_x) * 2 + rank
    slots = jnp.arange(16, dtype=jnp.int32)[:, None]
    stay = pick((slots == place[None, :]) & (to_c[None, :] == 0), rows)
    leave = pick((slots == place[None, :]) & (to_c[None, :] == 1), rows)
    arrived = shift(leave, "core", 1)
    kept = jnp.concatenate([stay[:8], arrived[:8]], axis=0)
    sent = after(jnp.concatenate([stay[8:], arrived[8:]], axis=0), gate)
    both = jnp.concatenate([kept, shift(sent, "group", 1)], axis=0)
    by_x = both.reshape(4, 4, 2, -1)
    groups = [by_x[:, k].reshape(8, -1) for k in range(4)]
    here = jnp.concatenate([groups[0], *(shift(groups[k], "x", k) for k in (1, 2, 3))], axis=0)
    source = jnp.arange(32, dtype=jnp.int32)
    k, sg, sc, r = source // 8, source // 4 % 2, source // 2 % 2, source % 2
    final = (((g + sg) % 2 * 4 + (x - k) % 4) * 2 + (c + sc) % 2) * 2 + r
    return pick(jnp.arange(32, dtype=jnp.int32)[:, None] == final[None, :], here)


def local(
    teacher_hidden,
    teacher_gain,
    project_weight,
    student_hidden,
    student_gain,
    gate_weight,
    up_weight,
    down_weight,
    owner_map,
    token_ids,
    token_counts,
    id_weight,
):
    episodes = token_counts.shape[0]
    hidden = gate_weight.shape[1]
    width = student_hidden.shape[1]
    block = width // 4
    position = lax.axis_index(TENSOR)
    tokens_all = EP_LEN * episodes * lax.axis_size(OWNERS)

    near = jnp.concatenate([down_weight.T, gate_weight, up_weight], axis=1)
    rows_each = near.shape[0]
    far_top = shift(near[: rows_each // 2], "group", 1)
    near_own = ring_pieces(near, "x")
    near_first, near_last = (near_own[1], near_own[4]), (near_own[2], near_own[3])
    near_other = swapped(near_own)
    top_own = ring_pieces(after(far_top, *near_last), "x")
    top_first, top_last = (top_own[1], top_own[4]), (top_own[2], top_own[3])
    top_other = swapped(top_own)

    student_hidden, teacher_hidden = after(student_hidden, near), after(teacher_hidden, near)
    wide = student_hidden.astype(F32)
    rescale = lax.rsqrt(jnp.mean(wide * wide, axis=1, keepdims=True) + EPSILON)
    normed = (wide * rescale * student_gain[None, :]).astype(BF16)
    both_rows = relative_columns(jnp.concatenate([normed, student_hidden], axis=0))
    student = both_rows[episodes:].astype(F32)
    widened = teacher_hidden.astype(F32)
    squares = jnp.sum(widened * widened, axis=1).reshape(EP_LEN, episodes).T
    column = jnp.concatenate([both_rows[:episodes], two_parts(squares)], axis=1)
    column = gather_z_doubling(after(column, far_top, *near_first))
    far_bottom = shift(after(near[rows_each // 2 :], column), "group", 1)
    bottom_own = ring_pieces(after(far_bottom, *top_last), "x")
    bottom_other = swapped(bottom_own)
    gathered_pieces = ring_pieces(column, "y", *top_first)
    gathered = jnp.concatenate(gathered_pieces, axis=0)
    totals = jnp.sum(gathered[:, width:].reshape(EP_LEN, episodes, -1).astype(F32), axis=0)
    totals = totals[:, :EP_LEN] + totals[:, EP_LEN : 2 * EP_LEN]
    totals = jnp.sum(jnp.where(jnp.arange(EP_LEN)[None, :] == position, totals, 0.0), axis=1)
    inverse = lax.rsqrt(totals / DT + EPSILON)

    teacher = teacher_hidden.reshape(4, 4, episodes, -1)
    teacher = rolled(crossed(teacher, 0, "z"), 1, "y").transpose(1, 0, 2, 3)
    widened = teacher.reshape(EP_LEN * episodes, -1).astype(F32)
    scaled = (widened * teacher_gain[None, :]).astype(BF16)
    share = EP_LEN * episodes // 4

    def part(low, rows, *gates):
        product = jnp.dot(scaled[low : low + rows], project_weight, preferred_element_type=F32)
        return after(product.astype(BF16), *gates)

    total = scatter_ring(
        part(0, share),
        part(share, share),
        part(2 * share, share // 2, *near_first),
        part(2 * share + share // 2, share // 2, *near_first),
        part(3 * share, share),
        "y",
        *near_first,
    )
    total = scatter_z_halving(after(total.astype(BF16), far_bottom), bottom_own[1], bottom_own[4])
    projected = (total * inverse[:, None]).astype(BF16)
    projected = relative_columns(projected).astype(F32)

    ids = jnp.arange(id_weight.shape[0], dtype=jnp.int32)
    looked = jnp.sum(jnp.where(token_ids[:, None] == ids[None, :], id_weight[None, :], 0.0), axis=1)
    weight = jnp.where(position < token_counts, looked, 0.0).astype(BF16).astype(F32)
    scale = 1.0 / math.sqrt(tokens_all)

    def starts(pieces, low):
        return ring_starts(pieces, rows_each, low) + ring_starts(pieces, rows_each, low + block)

    near_pieces, near_starts = near_own + near_other, starts(near_own, 0)
    near_sums = joined_product(gathered, near_pieces, near_starts, hidden)
    activated, far_branch, near_branch = feed_forward(
        gathered,
        after(near_sums, total),
        top_own + top_other + bottom_own + bottom_other,
        starts(top_own, 0) + starts(bottom_own, rows_each // 2),
        near_pieces,
        near_starts,
        hidden,
    )

    def gradient_half(far, branch_rows):
        columns = slice(far * 2 * block, (far + 1) * 2 * block)
        predicted = student[:, columns] + scatter_z(branch_rows)
        difference = predicted - projected[:, columns]
        return predicted, gather_z((weight[:, None] * difference * scale).astype(BF16))

    def owners_half(grad):
        mine, other = (
            jnp.einsum(
                "rc,rh->ch", grad[:, a : a + block], activated, preferred_element_type=F32
            ).astype(BF16)
            for a in (0, block)
        )
        both = mine + shift(other, "core", 1)
        quarter = block // 4
        blocks = [both[k * quarter // 2 : (k + 1) * quarter // 2] for k in range(8)]
        return scatter_ring(
            both[:quarter], both[quarter : 2 * quarter], blocks[4], blocks[5], both[3 * quarter :], "x"
        )

    far_rows = scatter_y(far_branch).astype(BF16)
    near_rows = scatter_y(near_branch).astype(BF16)
    far_predicted, far_column = gradient_half(1, far_rows)
    near_predicted, near_column = gradient_half(0, near_rows)
    far_grad = gather_y(far_column)
    near_grad = gather_y(near_column)
    far_reduced = owners_half(far_grad)
    near_reduced = owners_half(near_grad)
    down_grad = near_reduced + shift(far_reduced.astype(BF16), "group", 1).astype(F32)

    predicted = [near_predicted, far_predicted]
    rows = jnp.concatenate([p.astype(BF16) for p in predicted], axis=1)
    student_out = to_owners(absolute_columns(rows), owner_map, far_grad)
    return (student_out[None, None], down_grad)


def solution(mesh):
    split = Mesh(mesh.devices.reshape(*AXES.values()), tuple(AXES))
    placed = (
        P(OWNERS, TENSOR),
        P(TENSOR),
        P(TENSOR, None),
        P((*OWNERS, *TENSOR), None),
        P(),
        P(OWNERS, TENSOR),
        P(OWNERS, TENSOR),
        P(TENSOR, OWNERS),
        P(OWNERS, None),
        P((*OWNERS, *TENSOR)),
        P(OWNERS),
        P(),
    )
    return jax.shard_map(
        local,
        mesh=split,
        in_specs=placed,
        out_specs=(P(OWNERS, TENSOR, None, None), P(OWNERS, TENSOR)),
        check_vma=False,
    )
```

```python
import math

import jax
import jax.numpy as jnp
from jax import lax
from jax.experimental import pallas as pl
from jax.experimental.pallas import tpu as pltpu
from jax.sharding import Mesh
from jax.sharding import PartitionSpec as P

DT = 8192
EP_LEN = 16
AXES = {"group": 2, "x": 4, "core": 2, "z": 4, "y": 4}
OWNERS = ("group", "x", "core")
TENSOR = ("z", "y")
EPSILON = 1e-06
F32 = jnp.float32
BF16 = jnp.bfloat16


def shift(array, axis, by):
    size = AXES[axis]
    return lax.ppermute(array, axis, [(i, (i + by) % size) for i in range(size)])


def rolled(array, axis, name):
    doubled = jnp.concatenate([array, array], axis=axis)
    return lax.dynamic_slice_in_dim(doubled, lax.axis_index(name), array.shape[axis], axis)


def unrolled(array, axis, name):
    size = array.shape[axis]
    doubled = jnp.concatenate([array, array], axis=axis)
    return lax.dynamic_slice_in_dim(doubled, size - lax.axis_index(name), size, axis)


def exchange(array, axis, bits):
    return lax.ppermute(array, axis, [(i, i ^ bits) for i in range(AXES[axis])])


def relative_columns(rows):
    n = rows.shape[0]
    blocks = rows.reshape(n, 2, 4, 2, -1).transpose(1, 3, 2, 0, 4)
    blocks = rolled(rolled(rolled(blocks, 0, "group"), 1, "core"), 2, "x")
    return blocks.transpose(3, 0, 1, 2, 4).reshape(n, -1)


def absolute_columns(rows):
    n = rows.shape[0]
    blocks = rows.reshape(n, 2, 2, 4, -1).transpose(1, 2, 3, 0, 4)
    blocks = unrolled(unrolled(unrolled(blocks, 0, "group"), 1, "core"), 2, "x")
    return blocks.transpose(3, 0, 2, 1, 4).reshape(n, -1)


def after(array, *earlier):
    return lax.optimization_barrier((array, *earlier))[0]


def ring_pieces(piece, axis, *gates):
    half = (piece.shape[0] + 31) // 32 * 16
    behind = shift(piece, axis, 1)
    ahead = shift(piece, axis, -1)
    top = shift(after(behind[:half], *gates), axis, 1)
    bottom = shift(after(ahead[half:], *gates), axis, -1)
    return [piece, ahead, top, bottom, behind]


def swapped(pieces):
    return [shift(p, "core", 1) for p in pieces]


def ring_starts(pieces, block, low):
    return [low, low + block, low + 2 * block, low + 2 * block + pieces[2].shape[0], low + 3 * block]


def joined_product(rows, pieces, starts, skip):
    tokens, width, columns = rows.shape[0], sum(p.shape[0] for p in pieces), pieces[0].shape[1]
    count = len(pieces)

    def kernel(rows_ref, *refs):
        out_ref, whole, sems = refs[count:]
        copies = [
            pltpu.make_async_copy(refs[k], whole.at[pl.ds(starts[k], pieces[k].shape[0]), :], sems.at[k])
            for k in range(count)
        ]
        for c in copies:
            c.start()
        for c in copies:
            c.wait()
        total = jnp.dot(rows_ref[...], whole[...], preferred_element_type=F32)
        out_ref[...] = total[:, skip:]

    out = jax.ShapeDtypeStruct((tokens, columns - skip), F32)
    return pl.pallas_call(
        kernel,
        grid=(1,),
        in_specs=[
            pl.BlockSpec((tokens, width), lambda i: (0, 0)),
            *(pl.BlockSpec(memory_space=pltpu.HBM) for _ in pieces),
        ],
        out_specs=pl.BlockSpec(out.shape, lambda i: (0, 0)),
        out_shape=out,
        scratch_shapes=[pltpu.VMEM((width, columns), BF16), pltpu.SemaphoreType.DMA((count,))],
        compiler_params=pltpu.CompilerParams(vmem_limit_bytes=58 * 2**20),
    )(rows, *pieces)


def feed_forward(rows, near_sums, far, far_starts, near, near_starts, hidden):
    tokens, columns = rows.shape[0], far[0].shape[1]
    width = sum(p.shape[0] for p in far)
    lanes = -(-hidden // 128) * 128
    share = tokens // 4

    def kernel(rows_ref, near_sums_ref, *refs):
        far_refs, near_refs = refs[: len(far)], refs[len(far) : len(far) + len(near)]
        rest = refs[len(far) + len(near) :]
        activated_ref, far_outs, near_outs = rest[0], rest[1:5], rest[5:9]
        whole, near_down, padded, far_sems, near_sems = rest[9:]
        far_copies = [
            pltpu.make_async_copy(ref, whole.at[pl.ds(low, ref.shape[0]), :], far_sems.at[k])
            for k, (ref, low) in enumerate(zip(far_refs, far_starts))
        ]
        near_copies = [
            pltpu.make_async_copy(
                ref.at[:, pl.ds(0, lanes)], near_down.at[pl.ds(low, ref.shape[0]), :], near_sems.at[k]
            )
            for k, (ref, low) in enumerate(zip(near_refs, near_starts))
        ]
        for c in far_copies + near_copies:
            c.start()
        padded[...] = jnp.zeros_like(padded)
        for c in far_copies:
            c.wait()
        total = jnp.dot(rows_ref[...], whole[...], preferred_element_type=F32)[:, hidden:]
        total = total + near_sums_ref[...]
        gate, up = total[:, :hidden], total[:, hidden:]
        activated = (gate / (1.0 + jnp.exp(-gate)) * up).astype(BF16)
        activated_ref[...] = activated
        padded[:, :hidden] = activated
        for c in near_copies:
            c.wait()
        for down, outs in ((whole[:, :lanes], far_outs), (near_down[...], near_outs)):
            branch = lax.dot_general(
                padded[...], down, (((1,), (1,)), ((), ())), preferred_element_type=F32
            ).astype(BF16)
            for k, out in enumerate(outs):
                out[...] = branch[k * share : (k + 1) * share]

    block = jax.ShapeDtypeStruct((share, width), BF16)
    outs = [jax.ShapeDtypeStruct((tokens, hidden), BF16), *[block] * 8]
    activated, *blocks = pl.pallas_call(
        kernel,
        grid=(1,),
        in_specs=[
            pl.BlockSpec((tokens, width), lambda i: (0, 1)),
            pl.BlockSpec(near_sums.shape, lambda i: (0, 0)),
            *(pl.BlockSpec(memory_space=pltpu.HBM) for _ in far + near),
        ],
        out_specs=[pl.BlockSpec(o.shape, lambda i: (0, 0)) for o in outs],
        out_shape=outs,
        scratch_shapes=[
            pltpu.VMEM((width, columns), BF16),
            pltpu.VMEM((width, lanes), BF16),
            pltpu.VMEM((tokens, lanes), BF16),
            pltpu.SemaphoreType.DMA((len(far),)),
            pltpu.SemaphoreType.DMA((len(near),)),
        ],
        compiler_params=pltpu.CompilerParams(vmem_limit_bytes=58 * 2**20),
    )(rows, near_sums, *far, *near)
    return activated, blocks[:4], blocks[4:]


def teacher_parts(rows, gain, weight, positions):
    each = rows.shape[0] // EP_LEN
    share = rows.shape[0] // 4
    sizes = (share, share, share // 2, share // 2, share)

    def kernel(positions_ref, rows_ref, gain_ref, weight_ref, *rest):
        outs, scaled = rest[:-1], rest[-1]
        for k in range(EP_LEN):
            low = pl.multiple_of(positions_ref[k] * each, each)
            wide = rows_ref[pl.ds(low, each), :].astype(F32)
            scaled[k * each : (k + 1) * each, :] = (wide * gain_ref[...]).astype(BF16)
        product = jnp.dot(scaled[...], weight_ref[...], preferred_element_type=F32).astype(BF16)
        low = 0
        for out, size in zip(outs, sizes):
            out[...] = product[low : low + size]
            low += size

    return pl.pallas_call(
        kernel,
        in_specs=[
            pl.BlockSpec(memory_space=pltpu.SMEM),
            *(pl.BlockSpec(memory_space=pltpu.VMEM) for _ in range(3)),
        ],
        out_specs=[pl.BlockSpec(memory_space=pltpu.VMEM) for _ in sizes],
        out_shape=[jax.ShapeDtypeStruct((size, weight.shape[1]), BF16) for size in sizes],
        scratch_shapes=[pltpu.VMEM(rows.shape, BF16)],
        compiler_params=pltpu.CompilerParams(vmem_limit_bytes=40 * 2**20),
    )(positions, rows, gain[None, :], weight)


def gather_z(rows):
    return jnp.concatenate([rows, *(exchange(rows, "z", k) for k in (1, 2, 3))], axis=0)


def gather_z_doubling(rows):
    pair = jnp.concatenate([rows, exchange(rows, "z", 1)], axis=0)
    return jnp.concatenate([pair, exchange(pair, "z", 2)], axis=0)


def gather_y(rows):
    return jnp.concatenate([rows, *(shift(rows, "y", -k) for k in (1, 2, 3))], axis=0)


def added(parts, arrived):
    total = parts.astype(F32)
    for a in arrived:
        total = total + a.astype(F32)
    return total


def scatter_y(blocks):
    return added(blocks[0], [shift(blocks[k], "y", k) for k in (1, 2, 3)])


def scatter_z(parts):
    n = parts.shape[0] // 4
    return added(parts[:n], [exchange(parts[k * n : (k + 1) * n], "z", k) for k in (1, 2, 3)])


def scatter_z_halving(parts, *gates):
    n = parts.shape[0] // 4
    pair = added(parts[: 2 * n], [exchange(parts[2 * n :], "z", 2)])
    return added(pair[:n], [exchange(after(pair[n:].astype(BF16), *gates), "z", 1)])


def scatter_ring(own, first, top, bottom, third, axis, *gates):
    half = top.shape[0]
    top, bottom = shift(top, axis, 1), shift(bottom, axis, -1)
    up = jnp.concatenate([first[:half] + top, first[half:]], axis=0)
    down = jnp.concatenate([third[:half], third[half:] + bottom], axis=0)
    up, down = after(up, *gates), after(down, *gates)
    return added(own, [shift(up, axis, 1), shift(down, axis, -1)])


def two_parts(values):
    high = lax.reduce_precision(values, 8, 7)
    both = jnp.concatenate([high, values - high], axis=1).astype(BF16)
    return jnp.pad(both, ((0, 0), (0, 128 - both.shape[1])))


def pick(onehot, rows):
    return jnp.dot(onehot.astype(BF16), rows, preferred_element_type=F32).astype(BF16)


def to_owners(rows, owner_local, gate):
    owner = owner_local[:, 0]
    index = jnp.arange(owner.shape[0], dtype=jnp.int32)
    earlier = (owner[None, :] == owner[:, None]) & (index[None, :] < index[:, None])
    rank = jnp.sum(earlier.astype(jnp.int32), axis=1)
    g, x, c = (lax.axis_index(a) for a in OWNERS)
    to_c = (owner % 2 + c) % 2
    to_g = (owner // 8 + g) % 2
    to_x = (owner // 2 % 4 - x) % 4
    place = (to_g * 4 + to_x) * 2 + rank
    slots = jnp.arange(16, dtype=jnp.int32)[:, None]
    stay = pick((slots == place[None, :]) & (to_c[None, :] == 0), rows)
    leave = pick((slots == place[None, :]) & (to_c[None, :] == 1), rows)
    arrived = shift(leave, "core", 1)
    kept = jnp.concatenate([stay[:8], arrived[:8]], axis=0)
    sent = after(jnp.concatenate([stay[8:], arrived[8:]], axis=0), gate)
    both = jnp.concatenate([kept, shift(sent, "group", 1)], axis=0)
    by_x = both.reshape(4, 4, 2, -1)
    groups = [by_x[:, k].reshape(8, -1) for k in range(4)]
    here = jnp.concatenate([groups[0], *(shift(groups[k], "x", k) for k in (1, 2, 3))], axis=0)
    source = jnp.arange(32, dtype=jnp.int32)
    k, sg, sc, r = source // 8, source // 4 % 2, source // 2 % 2, source % 2
    final = (((g + sg) % 2 * 4 + (x - k) % 4) * 2 + (c + sc) % 2) * 2 + r
    return pick(jnp.arange(32, dtype=jnp.int32)[:, None] == final[None, :], here)


def local(
    teacher_hidden,
    teacher_gain,
    project_weight,
    student_hidden,
    student_gain,
    gate_weight,
    up_weight,
    down_weight,
    owner_map,
    token_ids,
    token_counts,
    id_weight,
):
    episodes = token_counts.shape[0]
    hidden = gate_weight.shape[1]
    width = student_hidden.shape[1]
    block = width // 4
    position = lax.axis_index(TENSOR)
    tokens_all = EP_LEN * episodes * lax.axis_size(OWNERS)

    near = jnp.concatenate([down_weight.T, gate_weight, up_weight], axis=1)
    rows_each = near.shape[0]
    near_far = shift(near, "group", 1)
    near_own = ring_pieces(near, "x")
    near_first, near_last = (near_own[1], near_own[4]), (near_own[2], near_own[3])
    near_other = swapped(near_own)
    far_own = ring_pieces(after(near_far, *near_other), "x")
    far_first = (far_own[1], far_own[4])
    far_other = swapped(far_own)

    student_hidden, teacher_hidden = after(student_hidden, near), after(teacher_hidden, near)
    wide = student_hidden.astype(F32)
    rescale = lax.rsqrt(jnp.mean(wide * wide, axis=1, keepdims=True) + EPSILON)
    normed = (wide * rescale * student_gain[None, :]).astype(BF16)
    both_rows = relative_columns(jnp.concatenate([normed, student_hidden], axis=0))
    student = both_rows[episodes:].astype(F32)
    widened = teacher_hidden.astype(F32)
    squares = jnp.sum(widened * widened, axis=1).reshape(EP_LEN, episodes).T
    column = jnp.concatenate([both_rows[:episodes], two_parts(squares)], axis=1)
    column = gather_z_doubling(after(column, near_far, *near_other))
    gathered_pieces = ring_pieces(after(column, *far_first, far_other[0]), "y", far_other[1], far_other[4])
    gathered = jnp.concatenate(gathered_pieces, axis=0)
    totals = jnp.sum(gathered[:, width:].reshape(EP_LEN, episodes, -1).astype(F32), axis=0)
    totals = totals[:, :EP_LEN] + totals[:, EP_LEN : 2 * EP_LEN]
    totals = jnp.sum(jnp.where(jnp.arange(EP_LEN)[None, :] == position, totals, 0.0), axis=1)
    inverse = lax.rsqrt(totals / DT + EPSILON)

    ahead = jnp.arange(EP_LEN, dtype=jnp.int32)
    positions = (lax.axis_index("z") ^ ahead % 4) * 4 + (lax.axis_index("y") + ahead // 4) % 4
    parts = teacher_parts(after(teacher_hidden, *near_last), teacher_gain, project_weight, positions)
    total = scatter_ring(*parts, "y")
    total = scatter_z_halving(after(total.astype(BF16), column), *far_first)
    projected = (total * inverse[:, None]).astype(BF16)
    projected = relative_columns(projected).astype(F32)

    ids = jnp.arange(id_weight.shape[0], dtype=jnp.int32)
    looked = jnp.sum(jnp.where(token_ids[:, None] == ids[None, :], id_weight[None, :], 0.0), axis=1)
    weight = jnp.where(position < token_counts, looked, 0.0).astype(BF16).astype(F32)
    scale = 1.0 / math.sqrt(tokens_all)

    def starts(pieces, low):
        return ring_starts(pieces, rows_each, low) + ring_starts(pieces, rows_each, low + block)

    near_pieces, near_starts = near_own + near_other, starts(near_own, 0)
    near_sums = joined_product(gathered, near_pieces, near_starts, hidden)
    activated, far_branch, near_branch = feed_forward(
        gathered,
        after(near_sums, total),
        far_own + far_other,
        starts(far_own, 0),
        near_pieces,
        near_starts,
        hidden,
    )

    def gradient_half(far, branch_rows):
        columns = slice(far * 2 * block, (far + 1) * 2 * block)
        predicted = student[:, columns] + scatter_z(branch_rows)
        difference = predicted - projected[:, columns]
        return predicted, gather_z((weight[:, None] * difference * scale).astype(BF16))

    def owners_half(grad):
        mine, other = (
            jnp.einsum(
                "rc,rh->ch", grad[:, a : a + block], activated, preferred_element_type=F32
            ).astype(BF16)
            for a in (0, block)
        )
        both = mine + shift(other, "core", 1)
        quarter = block // 4
        blocks = [both[k * quarter // 2 : (k + 1) * quarter // 2] for k in range(8)]
        return scatter_ring(
            both[:quarter], both[quarter : 2 * quarter], blocks[4], blocks[5], both[3 * quarter :], "x"
        )

    far_rows = scatter_y(far_branch).astype(BF16)
    near_rows = scatter_y(near_branch).astype(BF16)
    far_predicted, far_column = gradient_half(1, far_rows)
    near_predicted, near_column = gradient_half(0, near_rows)
    far_grad = gather_y(far_column)
    near_grad = gather_y(near_column)
    far_reduced = owners_half(far_grad)
    near_reduced = owners_half(near_grad)
    down_grad = near_reduced + shift(far_reduced.astype(BF16), "group", 1).astype(F32)

    predicted = [near_predicted, far_predicted]
    rows = jnp.concatenate([p.astype(BF16) for p in predicted], axis=1)
    student_out = to_owners(absolute_columns(rows), owner_map, far_grad)
    return (student_out[None, None], down_grad)


def solution(mesh):
    split = Mesh(mesh.devices.reshape(*AXES.values()), tuple(AXES))
    placed = (
        P(OWNERS, TENSOR),
        P(TENSOR),
        P(TENSOR, None),
        P((*OWNERS, *TENSOR), None),
        P(),
        P(OWNERS, TENSOR),
        P(OWNERS, TENSOR),
        P(TENSOR, OWNERS),
        P(OWNERS, None),
        P((*OWNERS, *TENSOR)),
        P(OWNERS),
        P(),
    )
    return jax.shard_map(
        local,
        mesh=split,
        in_specs=placed,
        out_specs=(P(OWNERS, TENSOR, None, None), P(OWNERS, TENSOR)),
        check_vma=False,
    )
```

```python
import math

import jax
import jax.numpy as jnp
from jax import lax
from jax.experimental import pallas as pl
from jax.experimental.pallas import tpu as pltpu
from jax.sharding import Mesh
from jax.sharding import PartitionSpec as P

DT = 8192
EP_LEN = 16
AXES = {"group": 2, "x": 4, "core": 2, "z": 4, "y": 4}
OWNERS = ("group", "x", "core")
TENSOR = ("z", "y")
EPSILON = 1e-06
F32 = jnp.float32
BF16 = jnp.bfloat16


def shift(array, axis, by):
    size = AXES[axis]
    return lax.ppermute(array, axis, [(i, (i + by) % size) for i in range(size)])


def rolled(array, axis, name):
    doubled = jnp.concatenate([array, array], axis=axis)
    return lax.dynamic_slice_in_dim(doubled, lax.axis_index(name), array.shape[axis], axis)


def unrolled(array, axis, name):
    size = array.shape[axis]
    doubled = jnp.concatenate([array, array], axis=axis)
    return lax.dynamic_slice_in_dim(doubled, size - lax.axis_index(name), size, axis)


def exchange(array, axis, bits):
    return lax.ppermute(array, axis, [(i, i ^ bits) for i in range(AXES[axis])])


def relative_columns(rows):
    n = rows.shape[0]
    blocks = rows.reshape(n, 2, 4, 2, -1).transpose(1, 3, 2, 0, 4)
    blocks = rolled(rolled(rolled(blocks, 0, "group"), 1, "core"), 2, "x")
    return blocks.transpose(3, 0, 1, 2, 4).reshape(n, -1)


def absolute_columns(rows):
    n = rows.shape[0]
    blocks = rows.reshape(n, 2, 2, 4, -1).transpose(1, 2, 3, 0, 4)
    blocks = unrolled(unrolled(unrolled(blocks, 0, "group"), 1, "core"), 2, "x")
    return blocks.transpose(3, 0, 2, 1, 4).reshape(n, -1)


def after(array, *earlier):
    return lax.optimization_barrier((array, *earlier))[0]


def ring_pieces(piece, axis, *gates):
    half = (piece.shape[0] + 31) // 32 * 16
    behind = shift(piece, axis, 1)
    ahead = shift(piece, axis, -1)
    top = shift(after(behind[:half], *gates), axis, 1)
    bottom = shift(after(ahead[half:], *gates), axis, -1)
    return [piece, ahead, top, bottom, behind]


def swapped(pieces):
    return [shift(p, "core", 1) for p in pieces]


def ring_starts(pieces, block, low):
    return [low, low + block, low + 2 * block, low + 2 * block + pieces[2].shape[0], low + 3 * block]


def joined_product(rows, pieces, starts, skip):
    tokens, width, columns = rows.shape[0], sum(p.shape[0] for p in pieces), pieces[0].shape[1]
    count = len(pieces)

    def kernel(rows_ref, *refs):
        out_ref, whole, sems = refs[count:]
        copies = [
            pltpu.make_async_copy(refs[k], whole.at[pl.ds(starts[k], pieces[k].shape[0]), :], sems.at[k])
            for k in range(count)
        ]
        for c in copies:
            c.start()
        total = None
        for core in range(2):
            for c in copies[core * count // 2 : (core + 1) * count // 2]:
                c.wait()
            span = slice(core * width // 2, (core + 1) * width // 2)
            part = jnp.dot(rows_ref[:, span], whole[span, :], preferred_element_type=F32)
            total = part if total is None else total + part
        out_ref[...] = total[:, skip:]

    out = jax.ShapeDtypeStruct((tokens, columns - skip), F32)
    return pl.pallas_call(
        kernel,
        grid=(1,),
        in_specs=[
            pl.BlockSpec((tokens, width), lambda i: (0, 0)),
            *(pl.BlockSpec(memory_space=pltpu.HBM) for _ in pieces),
        ],
        out_specs=pl.BlockSpec(out.shape, lambda i: (0, 0)),
        out_shape=out,
        scratch_shapes=[pltpu.VMEM((width, columns), BF16), pltpu.SemaphoreType.DMA((count,))],
        compiler_params=pltpu.CompilerParams(vmem_limit_bytes=58 * 2**20),
    )(rows, *pieces)


def feed_forward(rows, near_sums, far, far_starts, near, near_starts, hidden):
    tokens, columns = rows.shape[0], far[0].shape[1]
    width = sum(p.shape[0] for p in far)
    lanes = -(-hidden // 128) * 128
    share = tokens // 4

    def kernel(rows_ref, near_sums_ref, *refs):
        far_refs, near_refs = refs[: len(far)], refs[len(far) : len(far) + len(near)]
        rest = refs[len(far) + len(near) :]
        activated_ref, far_outs, near_outs = rest[0], rest[1:5], rest[5:9]
        whole, near_down, padded, far_sems, near_sems = rest[9:]
        far_copies = [
            pltpu.make_async_copy(ref, whole.at[pl.ds(low, ref.shape[0]), :], far_sems.at[k])
            for k, (ref, low) in enumerate(zip(far_refs, far_starts))
        ]
        near_copies = [
            pltpu.make_async_copy(
                ref.at[:, pl.ds(0, lanes)], near_down.at[pl.ds(low, ref.shape[0]), :], near_sems.at[k]
            )
            for k, (ref, low) in enumerate(zip(near_refs, near_starts))
        ]
        for c in far_copies + near_copies:
            c.start()
        padded[...] = jnp.zeros_like(padded)
        total = near_sums_ref[...]
        for core in range(2):
            for c in far_copies[core * len(far) // 2 : (core + 1) * len(far) // 2]:
                c.wait()
            span = slice(core * width // 2, (core + 1) * width // 2)
            part = jnp.dot(rows_ref[:, span], whole[span, :], preferred_element_type=F32)
            total = total + part[:, hidden:]
        gate, up = total[:, :hidden], total[:, hidden:]
        activated = (gate / (1.0 + jnp.exp(-gate)) * up).astype(BF16)
        activated_ref[...] = activated
        padded[:, :hidden] = activated
        for c in near_copies:
            c.wait()
        for down, outs in ((whole[:, :lanes], far_outs), (near_down[...], near_outs)):
            branch = lax.dot_general(
                padded[...], down, (((1,), (1,)), ((), ())), preferred_element_type=F32
            ).astype(BF16)
            for k, out in enumerate(outs):
                out[...] = branch[k * share : (k + 1) * share]

    block = jax.ShapeDtypeStruct((share, width), BF16)
    outs = [jax.ShapeDtypeStruct((tokens, hidden), BF16), *[block] * 8]
    activated, *blocks = pl.pallas_call(
        kernel,
        grid=(1,),
        in_specs=[
            pl.BlockSpec((tokens, width), lambda i: (0, 1)),
            pl.BlockSpec(near_sums.shape, lambda i: (0, 0)),
            *(pl.BlockSpec(memory_space=pltpu.HBM) for _ in far + near),
        ],
        out_specs=[pl.BlockSpec(o.shape, lambda i: (0, 0)) for o in outs],
        out_shape=outs,
        scratch_shapes=[
            pltpu.VMEM((width, columns), BF16),
            pltpu.VMEM((width, lanes), BF16),
            pltpu.VMEM((tokens, lanes), BF16),
            pltpu.SemaphoreType.DMA((len(far),)),
            pltpu.SemaphoreType.DMA((len(near),)),
        ],
        compiler_params=pltpu.CompilerParams(vmem_limit_bytes=58 * 2**20),
    )(rows, near_sums, *far, *near)
    return activated, blocks[:4], blocks[4:]


def teacher_parts(rows, gain, weight, positions):
    each = rows.shape[0] // EP_LEN
    share = rows.shape[0] // 4
    sizes = (share, share, share // 2, share // 2, share)

    def kernel(positions_ref, rows_ref, gain_ref, weight_ref, *rest):
        outs, scaled = rest[:-1], rest[-1]
        for k in range(EP_LEN):
            low = pl.multiple_of(positions_ref[k] * each, each)
            wide = rows_ref[pl.ds(low, each), :].astype(F32)
            scaled[k * each : (k + 1) * each, :] = (wide * gain_ref[...]).astype(BF16)
        product = jnp.dot(scaled[...], weight_ref[...], preferred_element_type=F32).astype(BF16)
        low = 0
        for out, size in zip(outs, sizes):
            out[...] = product[low : low + size]
            low += size

    return pl.pallas_call(
        kernel,
        in_specs=[
            pl.BlockSpec(memory_space=pltpu.SMEM),
            *(pl.BlockSpec(memory_space=pltpu.VMEM) for _ in range(3)),
        ],
        out_specs=[pl.BlockSpec(memory_space=pltpu.VMEM) for _ in sizes],
        out_shape=[jax.ShapeDtypeStruct((size, weight.shape[1]), BF16) for size in sizes],
        scratch_shapes=[pltpu.VMEM(rows.shape, BF16)],
        compiler_params=pltpu.CompilerParams(vmem_limit_bytes=40 * 2**20),
    )(positions, rows, gain[None, :], weight)


def gather_z(rows):
    return jnp.concatenate([rows, *(exchange(rows, "z", k) for k in (1, 2, 3))], axis=0)


def gather_z_doubling(rows):
    pair = jnp.concatenate([rows, exchange(rows, "z", 1)], axis=0)
    return jnp.concatenate([pair, exchange(pair, "z", 2)], axis=0)


def added(parts, arrived):
    total = parts.astype(F32)
    for a in arrived:
        total = total + a.astype(F32)
    return total


def scatter_y(blocks):
    return added(blocks[0], [shift(blocks[k], "y", k) for k in (1, 2, 3)])


def scatter_z(parts):
    n = parts.shape[0] // 4
    return added(parts[:n], [exchange(parts[k * n : (k + 1) * n], "z", k) for k in (1, 2, 3)])


def scatter_z_halving(parts, *gates):
    n = parts.shape[0] // 4
    pair = added(parts[: 2 * n], [exchange(parts[2 * n :], "z", 2)])
    return added(pair[:n], [exchange(after(pair[n:].astype(BF16), *gates), "z", 1)])


def scatter_ring(own, first, top, bottom, third, axis, *gates):
    half = top.shape[0]
    top, bottom = shift(top, axis, 1), shift(bottom, axis, -1)
    up = jnp.concatenate([first[:half] + top, first[half:]], axis=0)
    down = jnp.concatenate([third[:half], third[half:] + bottom], axis=0)
    up, down = after(up, *gates), after(down, *gates)
    return added(own, [shift(up, axis, 1), shift(down, axis, -1)])


def two_parts(values):
    high = lax.reduce_precision(values, 8, 7)
    both = jnp.concatenate([high, values - high], axis=1).astype(BF16)
    return jnp.pad(both, ((0, 0), (0, 128 - both.shape[1])))


def pick(onehot, rows):
    return jnp.dot(onehot.astype(BF16), rows, preferred_element_type=F32).astype(BF16)


def to_owners(rows, owner_local, gate):
    owner = owner_local[:, 0]
    index = jnp.arange(owner.shape[0], dtype=jnp.int32)
    earlier = (owner[None, :] == owner[:, None]) & (index[None, :] < index[:, None])
    rank = jnp.sum(earlier.astype(jnp.int32), axis=1)
    g, x, c = (lax.axis_index(a) for a in OWNERS)
    to_c = (owner % 2 + c) % 2
    to_g = (owner // 8 + g) % 2
    to_x = (owner // 2 % 4 - x) % 4
    place = (to_g * 4 + to_x) * 2 + rank
    slots = jnp.arange(16, dtype=jnp.int32)[:, None]
    stay = pick((slots == place[None, :]) & (to_c[None, :] == 0), rows)
    leave = pick((slots == place[None, :]) & (to_c[None, :] == 1), rows)
    arrived = shift(leave, "core", 1)
    kept = jnp.concatenate([stay[:8], arrived[:8]], axis=0)
    sent = after(jnp.concatenate([stay[8:], arrived[8:]], axis=0), gate)
    both = jnp.concatenate([kept, shift(sent, "group", 1)], axis=0)
    place = jnp.arange(32, dtype=jnp.int32)
    by_x = pick((place // 2 % 4 * 4 + place // 8) * 2 + place % 2 == place[:, None], both)
    groups = [by_x[8 * k : 8 * (k + 1)] for k in range(4)]
    here = jnp.concatenate([groups[0], *(shift(groups[k], "x", k) for k in (1, 2, 3))], axis=0)
    source = jnp.arange(32, dtype=jnp.int32)
    k, sg, sc, r = source // 8, source // 4 % 2, source // 2 % 2, source % 2
    final = (((g + sg) % 2 * 4 + (x - k) % 4) * 2 + (c + sc) % 2) * 2 + r
    return pick(jnp.arange(32, dtype=jnp.int32)[:, None] == final[None, :], here)


def local(
    teacher_hidden,
    teacher_gain,
    project_weight,
    student_hidden,
    student_gain,
    gate_weight,
    up_weight,
    down_weight,
    owner_map,
    token_ids,
    token_counts,
    id_weight,
):
    episodes = token_counts.shape[0]
    hidden = gate_weight.shape[1]
    width = student_hidden.shape[1]
    block = width // 4
    position = lax.axis_index(TENSOR)
    tokens_all = EP_LEN * episodes * lax.axis_size(OWNERS)

    near = jnp.concatenate([down_weight.T, gate_weight, up_weight], axis=1)
    rows_each = near.shape[0]
    near_far = shift(near, "group", 1)
    near_own = ring_pieces(near, "x")
    near_first, near_last = (near_own[1], near_own[4]), (near_own[2], near_own[3])
    near_other = swapped(near_own)
    far_own = ring_pieces(after(near_far, *near_other), "x")
    far_first = (far_own[1], far_own[4])
    far_other = swapped(far_own)

    student_hidden, teacher_hidden = after(student_hidden, near), after(teacher_hidden, near)
    wide = student_hidden.astype(F32)
    rescale = lax.rsqrt(jnp.mean(wide * wide, axis=1, keepdims=True) + EPSILON)
    normed = (wide * rescale * student_gain[None, :]).astype(BF16)
    both_rows = relative_columns(jnp.concatenate([normed, student_hidden], axis=0))
    student = both_rows[episodes:].astype(F32)
    widened = teacher_hidden.astype(F32)
    squares = jnp.sum(widened * widened, axis=1).reshape(EP_LEN, episodes).T
    column = jnp.concatenate([both_rows[:episodes], two_parts(squares)], axis=1)
    column = gather_z_doubling(after(column, near_far, *near_other))
    gathered_pieces = ring_pieces(after(column, *far_first, far_other[0]), "y", far_other[1], far_other[4])
    gathered = jnp.concatenate(gathered_pieces, axis=0)
    totals = jnp.sum(gathered[:, width:].reshape(EP_LEN, episodes, -1).astype(F32), axis=0)
    totals = totals[:, :EP_LEN] + totals[:, EP_LEN : 2 * EP_LEN]
    totals = jnp.sum(jnp.where(jnp.arange(EP_LEN)[None, :] == position, totals, 0.0), axis=1)
    inverse = lax.rsqrt(totals / DT + EPSILON)

    ahead = jnp.arange(EP_LEN, dtype=jnp.int32)
    positions = (lax.axis_index("z") ^ ahead % 4) * 4 + (lax.axis_index("y") + ahead // 4) % 4
    parts = teacher_parts(after(teacher_hidden, *near_last), teacher_gain, project_weight, positions)
    parts = [after(p, near_far, *near_other) for p in parts]
    total = scatter_ring(*parts, "y")
    total = scatter_z_halving(after(total.astype(BF16), far_own[2], far_own[3]))
    projected = (total * inverse[:, None]).astype(BF16)
    projected = relative_columns(projected).astype(F32)

    ids = jnp.arange(id_weight.shape[0], dtype=jnp.int32)
    looked = jnp.sum(jnp.where(token_ids[:, None] == ids[None, :], id_weight[None, :], 0.0), axis=1)
    weight = jnp.where(position < token_counts, looked, 0.0).astype(BF16).astype(F32)
    scale = 1.0 / math.sqrt(tokens_all)

    def starts(pieces, low):
        return ring_starts(pieces, rows_each, low) + ring_starts(pieces, rows_each, low + block)

    near_pieces, near_starts = near_own + near_other, starts(near_own, 0)
    near_sums = joined_product(gathered, near_pieces, near_starts, hidden)
    activated, far_branch, near_branch = feed_forward(
        gathered,
        after(near_sums, total),
        far_own + far_other,
        starts(far_own, 0),
        near_pieces,
        near_starts,
        hidden,
    )

    def gradient_half(far, branch_rows):
        columns = slice(far * 2 * block, (far + 1) * 2 * block)
        predicted = student[:, columns] + scatter_z(branch_rows)
        difference = predicted - projected[:, columns]
        return predicted, gather_z((weight[:, None] * difference * scale).astype(BF16))

    def owners_half(grad):
        mine, other = (
            jnp.einsum(
                "rc,rh->ch", grad[:, a : a + block], activated, preferred_element_type=F32
            ).astype(BF16)
            for a in (0, block)
        )
        both = mine + shift(other, "core", 1)
        quarter = block // 4
        blocks = [both[k * quarter // 2 : (k + 1) * quarter // 2] for k in range(8)]
        return scatter_ring(
            both[:quarter], both[quarter : 2 * quarter], blocks[4], blocks[5], both[3 * quarter :], "x"
        )

    far_rows = scatter_y(far_branch).astype(BF16)
    near_rows = scatter_y(near_branch).astype(BF16)
    far_predicted, far_column = gradient_half(1, far_rows)
    near_predicted, near_column = gradient_half(0, near_rows)
    far_ring, near_ring = ring_pieces(far_column, "y"), ring_pieces(near_column, "y")
    far_grad, near_grad = jnp.concatenate(far_ring, axis=0), jnp.concatenate(near_ring, axis=0)
    far_reduced = owners_half(far_grad)
    near_reduced = owners_half(near_grad)
    down_grad = near_reduced + shift(far_reduced.astype(BF16), "group", 1).astype(F32)

    predicted = [near_predicted, far_predicted]
    rows = jnp.concatenate([p.astype(BF16) for p in predicted], axis=1)
    student_out = to_owners(absolute_columns(rows), owner_map, far_ring[1])
    return (student_out[None, None], down_grad)


def solution(mesh):
    split = Mesh(mesh.devices.reshape(*AXES.values()), tuple(AXES))
    placed = (
        P(OWNERS, TENSOR),
        P(TENSOR),
        P(TENSOR, None),
        P((*OWNERS, *TENSOR), None),
        P(),
        P(OWNERS, TENSOR),
        P(OWNERS, TENSOR),
        P(TENSOR, OWNERS),
        P(OWNERS, None),
        P((*OWNERS, *TENSOR)),
        P(OWNERS),
        P(),
    )
    return jax.shard_map(
        local,
        mesh=split,
        in_specs=placed,
        out_specs=(P(OWNERS, TENSOR, None, None), P(OWNERS, TENSOR)),
        check_vma=False,
    )
```

```python
import math

import jax
import jax.numpy as jnp
from jax import lax
from jax.experimental import pallas as pl
from jax.experimental.pallas import tpu as pltpu
from jax.sharding import Mesh
from jax.sharding import PartitionSpec as P

DT = 8192
EP_LEN = 16
AXES = {"group": 2, "x": 4, "core": 2, "z": 4, "y": 4}
OWNERS = ("group", "x", "core")
TENSOR = ("z", "y")
EPSILON = 1e-06
F32 = jnp.float32
BF16 = jnp.bfloat16


def shift(array, axis, by):
    size = AXES[axis]
    return lax.ppermute(array, axis, [(i, (i + by) % size) for i in range(size)])


def rolled(array, axis, name):
    doubled = jnp.concatenate([array, array], axis=axis)
    return lax.dynamic_slice_in_dim(doubled, lax.axis_index(name), array.shape[axis], axis)


def unrolled(array, axis, name):
    size = array.shape[axis]
    doubled = jnp.concatenate([array, array], axis=axis)
    return lax.dynamic_slice_in_dim(doubled, size - lax.axis_index(name), size, axis)


def exchange(array, axis, bits):
    return lax.ppermute(array, axis, [(i, i ^ bits) for i in range(AXES[axis])])


def relative_columns(rows):
    n = rows.shape[0]
    blocks = rows.reshape(n, 2, 4, 2, -1).transpose(1, 3, 2, 0, 4)
    blocks = rolled(rolled(rolled(blocks, 0, "group"), 1, "core"), 2, "x")
    return blocks.transpose(3, 0, 1, 2, 4).reshape(n, -1)


def absolute_columns(rows):
    n = rows.shape[0]
    blocks = rows.reshape(n, 2, 2, 4, -1).transpose(1, 2, 3, 0, 4)
    blocks = unrolled(unrolled(unrolled(blocks, 0, "group"), 1, "core"), 2, "x")
    return blocks.transpose(3, 0, 2, 1, 4).reshape(n, -1)


def after(array, *earlier):
    return lax.optimization_barrier((array, *earlier))[0]


def ring_pieces(piece, axis, *gates):
    half = (piece.shape[0] + 31) // 32 * 16
    behind = shift(piece, axis, 1)
    ahead = shift(piece, axis, -1)
    top = shift(after(behind[:half], *gates), axis, 1)
    bottom = shift(after(ahead[half:], *gates), axis, -1)
    return [piece, ahead, top, bottom, behind]


def swapped(pieces):
    return [shift(p, "core", 1) for p in pieces]


def ring_starts(pieces, block, low):
    return [low, low + block, low + 2 * block, low + 2 * block + pieces[2].shape[0], low + 3 * block]


def feed_forward(rows, pieces, starts, hidden):
    tokens, columns = rows.shape[0], pieces[0].shape[1]
    width = sum(p.shape[0] for p in pieces)
    lanes = -(-hidden // 128) * 128
    count, groups = len(pieces), 4
    share = tokens // 4

    def kernel(rows_ref, *refs):
        activated_ref, outs = refs[count], refs[count + 1 : count + 9]
        whole, padded, sems = refs[count + 9 :]
        copies = [
            pltpu.make_async_copy(ref, whole.at[pl.ds(low, ref.shape[0]), :], sems.at[k])
            for k, (ref, low) in enumerate(zip(refs[:count], starts))
        ]
        for c in copies:
            c.start()
        padded[...] = jnp.zeros_like(padded)
        total = None
        for group in range(groups):
            for c in copies[group * count // groups : (group + 1) * count // groups]:
                c.wait()
            span = slice(group * width // groups, (group + 1) * width // groups)
            part = jnp.dot(rows_ref[:, span], whole[span, :], preferred_element_type=F32)
            total = part if total is None else total + part
        gate, up = total[:, hidden : 2 * hidden], total[:, 2 * hidden :]
        activated = (gate / (1.0 + jnp.exp(-gate)) * up).astype(BF16)
        activated_ref[...] = activated
        padded[:, :hidden] = activated
        for k in range(2):
            down = whole[k * width // 2 : (k + 1) * width // 2, :lanes]
            branch = lax.dot_general(
                padded[...], down, (((1,), (1,)), ((), ())), preferred_element_type=F32
            ).astype(BF16)
            for r in range(4):
                outs[4 * k + r][...] = branch[r * share : (r + 1) * share]

    block = jax.ShapeDtypeStruct((share, width // 2), BF16)
    out_shapes = [jax.ShapeDtypeStruct((tokens, hidden), BF16), *[block] * 8]
    activated, *blocks = pl.pallas_call(
        kernel,
        grid=(1,),
        in_specs=[
            pl.BlockSpec(rows.shape, lambda i: (0, 0)),
            *(pl.BlockSpec(memory_space=pltpu.HBM) for _ in pieces),
        ],
        out_specs=[pl.BlockSpec(o.shape, lambda i: (0, 0)) for o in out_shapes],
        out_shape=out_shapes,
        scratch_shapes=[
            pltpu.VMEM((width, columns), BF16),
            pltpu.VMEM((tokens, lanes), BF16),
            pltpu.SemaphoreType.DMA((count,)),
        ],
        compiler_params=pltpu.CompilerParams(vmem_limit_bytes=58 * 2**20),
    )(rows, *pieces)
    return activated, blocks[:4], blocks[4:]


def teacher_parts(rows, gain, weight, positions):
    each = rows.shape[0] // EP_LEN
    share = rows.shape[0] // 4
    sizes = (share, share, share // 2, share // 2, share)

    def kernel(positions_ref, rows_ref, gain_ref, weight_ref, *rest):
        outs, scaled = rest[:-1], rest[-1]
        for k in range(EP_LEN):
            low = pl.multiple_of(positions_ref[k] * each, each)
            wide = rows_ref[pl.ds(low, each), :].astype(F32)
            scaled[k * each : (k + 1) * each, :] = (wide * gain_ref[...]).astype(BF16)
        product = jnp.dot(scaled[...], weight_ref[...], preferred_element_type=F32).astype(BF16)
        low = 0
        for out, size in zip(outs, sizes):
            out[...] = product[low : low + size]
            low += size

    return pl.pallas_call(
        kernel,
        in_specs=[
            pl.BlockSpec(memory_space=pltpu.SMEM),
            *(pl.BlockSpec(memory_space=pltpu.VMEM) for _ in range(3)),
        ],
        out_specs=[pl.BlockSpec(memory_space=pltpu.VMEM) for _ in sizes],
        out_shape=[jax.ShapeDtypeStruct((size, weight.shape[1]), BF16) for size in sizes],
        scratch_shapes=[pltpu.VMEM(rows.shape, BF16)],
        compiler_params=pltpu.CompilerParams(vmem_limit_bytes=40 * 2**20),
    )(positions, rows, gain[None, :], weight)


def gather_z(rows):
    return jnp.concatenate([rows, *(exchange(rows, "z", k) for k in (1, 2, 3))], axis=0)


def gather_z_doubling(rows):
    pair = jnp.concatenate([rows, exchange(rows, "z", 1)], axis=0)
    return jnp.concatenate([pair, exchange(pair, "z", 2)], axis=0)


def added(parts, arrived):
    total = parts.astype(F32)
    for a in arrived:
        total = total + a.astype(F32)
    return total


def scatter_y(blocks):
    return added(blocks[0], [shift(blocks[k], "y", k) for k in (1, 2, 3)])


def scatter_z(parts):
    n = parts.shape[0] // 4
    return added(parts[:n], [exchange(parts[k * n : (k + 1) * n], "z", k) for k in (1, 2, 3)])


def scatter_z_halving(parts, *gates):
    n = parts.shape[0] // 4
    pair = added(parts[: 2 * n], [exchange(parts[2 * n :], "z", 2)])
    return added(pair[:n], [exchange(after(pair[n:].astype(BF16), *gates), "z", 1)])


def scatter_ring(own, first, top, bottom, third, axis, *gates):
    half = top.shape[0]
    top, bottom = shift(top, axis, 1), shift(bottom, axis, -1)
    up = jnp.concatenate([first[:half] + top, first[half:]], axis=0)
    down = jnp.concatenate([third[:half], third[half:] + bottom], axis=0)
    up, down = after(up, *gates), after(down, *gates)
    return added(own, [shift(up, axis, 1), shift(down, axis, -1)])


def two_parts(values):
    high = lax.reduce_precision(values, 8, 7)
    both = jnp.concatenate([high, values - high], axis=1).astype(BF16)
    return jnp.pad(both, ((0, 0), (0, 128 - both.shape[1])))


def pick(onehot, rows):
    return jnp.dot(onehot.astype(BF16), rows, preferred_element_type=F32).astype(BF16)


def to_owners(rows, owner_local, gate):
    owner = owner_local[:, 0]
    index = jnp.arange(owner.shape[0], dtype=jnp.int32)
    earlier = (owner[None, :] == owner[:, None]) & (index[None, :] < index[:, None])
    rank = jnp.sum(earlier.astype(jnp.int32), axis=1)
    g, x, c = (lax.axis_index(a) for a in OWNERS)
    to_c = (owner % 2 + c) % 2
    to_g = (owner // 8 + g) % 2
    to_x = (owner // 2 % 4 - x) % 4
    place = (to_g * 4 + to_x) * 2 + rank
    slots = jnp.arange(16, dtype=jnp.int32)[:, None]
    stay = pick((slots == place[None, :]) & (to_c[None, :] == 0), rows)
    leave = pick((slots == place[None, :]) & (to_c[None, :] == 1), rows)
    arrived = shift(leave, "core", 1)
    kept = jnp.concatenate([stay[:8], arrived[:8]], axis=0)
    sent = after(jnp.concatenate([stay[8:], arrived[8:]], axis=0), gate)
    both = jnp.concatenate([kept, shift(sent, "group", 1)], axis=0)
    place = jnp.arange(32, dtype=jnp.int32)
    by_x = pick((place // 2 % 4 * 4 + place // 8) * 2 + place % 2 == place[:, None], both)
    groups = [by_x[8 * k : 8 * (k + 1)] for k in range(4)]
    here = jnp.concatenate([groups[0], *(shift(groups[k], "x", k) for k in (1, 2, 3))], axis=0)
    source = jnp.arange(32, dtype=jnp.int32)
    k, sg, sc, r = source // 8, source // 4 % 2, source // 2 % 2, source % 2
    final = (((g + sg) % 2 * 4 + (x - k) % 4) * 2 + (c + sc) % 2) * 2 + r
    return pick(jnp.arange(32, dtype=jnp.int32)[:, None] == final[None, :], here)


def local(
    teacher_hidden,
    teacher_gain,
    project_weight,
    student_hidden,
    student_gain,
    gate_weight,
    up_weight,
    down_weight,
    owner_map,
    token_ids,
    token_counts,
    id_weight,
):
    episodes = token_counts.shape[0]
    hidden = gate_weight.shape[1]
    width = student_hidden.shape[1]
    block = width // 4
    position = lax.axis_index(TENSOR)
    tokens_all = EP_LEN * episodes * lax.axis_size(OWNERS)

    near = jnp.concatenate([down_weight.T, gate_weight, up_weight], axis=1)
    rows_each = near.shape[0]
    near_far = shift(near, "group", 1)
    near_own = ring_pieces(near, "x")
    near_first, near_last = (near_own[1], near_own[4]), (near_own[2], near_own[3])
    ahead = jnp.arange(EP_LEN, dtype=jnp.int32)
    positions = (lax.axis_index("z") ^ ahead % 4) * 4 + (lax.axis_index("y") + ahead // 4) % 4
    near_across = shift(near, "core", 1)
    rows = after(teacher_hidden, near_across, *near_first)
    parts = teacher_parts(rows, teacher_gain, project_weight, positions)
    near_relayed = [after(p, parts[0]) for p in near_last]
    near_other = [near_across, *swapped([near_own[1], *near_relayed, near_own[4]])]
    far_own = ring_pieces(after(near_far, *near_other), "x")
    far_first = (far_own[1], far_own[4])
    far_other = swapped(far_own)

    student_hidden, teacher_hidden = after(student_hidden, near), after(teacher_hidden, near)
    wide = student_hidden.astype(F32)
    rescale = lax.rsqrt(jnp.mean(wide * wide, axis=1, keepdims=True) + EPSILON)
    normed = (wide * rescale * student_gain[None, :]).astype(BF16)
    both_rows = relative_columns(jnp.concatenate([normed, student_hidden], axis=0))
    student = both_rows[episodes:].astype(F32)
    widened = teacher_hidden.astype(F32)
    squares = jnp.sum(widened * widened, axis=1).reshape(EP_LEN, episodes).T
    column = jnp.concatenate([both_rows[:episodes], two_parts(squares)], axis=1)
    column = gather_z_doubling(after(column, far_other[0], *near_other))
    gathered_pieces = ring_pieces(after(column, *far_first, far_other[0]), "y", far_other[1], far_other[4])
    gathered = jnp.concatenate(gathered_pieces, axis=0)
    totals = jnp.sum(gathered[:, width:].reshape(EP_LEN, episodes, -1).astype(F32), axis=0)
    totals = totals[:, :EP_LEN] + totals[:, EP_LEN : 2 * EP_LEN]
    totals = jnp.sum(jnp.where(jnp.arange(EP_LEN)[None, :] == position, totals, 0.0), axis=1)
    inverse = lax.rsqrt(totals / DT + EPSILON)

    total = scatter_ring(*parts, "y")
    total = scatter_z_halving(after(total.astype(BF16), far_own[2], far_own[3]))
    projected = (total * inverse[:, None]).astype(BF16)
    projected = relative_columns(projected).astype(F32)

    ids = jnp.arange(id_weight.shape[0], dtype=jnp.int32)
    looked = jnp.sum(jnp.where(token_ids[:, None] == ids[None, :], id_weight[None, :], 0.0), axis=1)
    weight = jnp.where(position < token_counts, looked, 0.0).astype(BF16).astype(F32)
    scale = 1.0 / math.sqrt(tokens_all)

    def starts(pieces, low):
        return ring_starts(pieces, rows_each, low) + ring_starts(pieces, rows_each, low + block)

    activated, near_branch, far_branch = feed_forward(
        after(gathered, total),
        near_own + near_other + far_own + far_other,
        starts(near_own, 0) + starts(far_own, 2 * block),
        hidden,
    )

    def gradient_half(far, branch_rows):
        columns = slice(far * 2 * block, (far + 1) * 2 * block)
        predicted = student[:, columns] + scatter_z(branch_rows)
        difference = predicted - projected[:, columns]
        return predicted, gather_z((weight[:, None] * difference * scale).astype(BF16))

    def owners_half(grad):
        mine, other = (
            jnp.einsum(
                "rc,rh->ch", grad[:, a : a + block], activated, preferred_element_type=F32
            ).astype(BF16)
            for a in (0, block)
        )
        both = mine + shift(other, "core", 1)
        quarter = block // 4
        blocks = [both[k * quarter // 2 : (k + 1) * quarter // 2] for k in range(8)]
        return scatter_ring(
            both[:quarter], both[quarter : 2 * quarter], blocks[4], blocks[5], both[3 * quarter :], "x"
        )

    far_rows = scatter_y(far_branch).astype(BF16)
    near_rows = scatter_y(near_branch).astype(BF16)
    far_predicted, far_column = gradient_half(1, far_rows)
    near_predicted, near_column = gradient_half(0, near_rows)
    far_ring, near_ring = ring_pieces(far_column, "y"), ring_pieces(near_column, "y")
    far_grad, near_grad = jnp.concatenate(far_ring, axis=0), jnp.concatenate(near_ring, axis=0)
    far_reduced = owners_half(far_grad)
    near_reduced = owners_half(near_grad)
    down_grad = near_reduced + shift(far_reduced.astype(BF16), "group", 1).astype(F32)

    predicted = [near_predicted, far_predicted]
    rows = jnp.concatenate([p.astype(BF16) for p in predicted], axis=1)
    student_out = to_owners(absolute_columns(rows), owner_map, far_ring[1])
    return (student_out[None, None], down_grad)


def solution(mesh):
    split = Mesh(mesh.devices.reshape(*AXES.values()), tuple(AXES))
    placed = (
        P(OWNERS, TENSOR),
        P(TENSOR),
        P(TENSOR, None),
        P((*OWNERS, *TENSOR), None),
        P(),
        P(OWNERS, TENSOR),
        P(OWNERS, TENSOR),
        P(TENSOR, OWNERS),
        P(OWNERS, None),
        P((*OWNERS, *TENSOR)),
        P(OWNERS),
        P(),
    )
    return jax.shard_map(
        local,
        mesh=split,
        in_specs=placed,
        out_specs=(P(OWNERS, TENSOR, None, None), P(OWNERS, TENSOR)),
        check_vma=False,
    )
```

```python
import math

import jax
import jax.numpy as jnp
from jax import lax
from jax.experimental import pallas as pl
from jax.experimental.pallas import tpu as pltpu
from jax.sharding import Mesh
from jax.sharding import PartitionSpec as P

DT = 8192
EP_LEN = 16
AXES = {"group": 2, "x": 4, "core": 2, "z": 4, "y": 4}
OWNERS = ("group", "x", "core")
TENSOR = ("z", "y")
EPSILON = 1e-06
F32 = jnp.float32
BF16 = jnp.bfloat16


def shift(array, axis, by):
    size = AXES[axis]
    return lax.ppermute(array, axis, [(i, (i + by) % size) for i in range(size)])


def rolled(array, axis, name):
    doubled = jnp.concatenate([array, array], axis=axis)
    return lax.dynamic_slice_in_dim(doubled, lax.axis_index(name), array.shape[axis], axis)


def unrolled(array, axis, name):
    size = array.shape[axis]
    doubled = jnp.concatenate([array, array], axis=axis)
    return lax.dynamic_slice_in_dim(doubled, size - lax.axis_index(name), size, axis)


def exchange(array, axis, bits):
    return lax.ppermute(array, axis, [(i, i ^ bits) for i in range(AXES[axis])])


def relative_columns(rows):
    n = rows.shape[0]
    blocks = rows.reshape(n, 2, 4, 2, -1).transpose(1, 3, 2, 0, 4)
    blocks = rolled(rolled(rolled(blocks, 0, "group"), 1, "core"), 2, "x")
    return blocks.transpose(3, 0, 1, 2, 4).reshape(n, -1)


def absolute_columns(rows):
    n = rows.shape[0]
    blocks = rows.reshape(n, 2, 2, 4, -1).transpose(1, 2, 3, 0, 4)
    blocks = unrolled(unrolled(unrolled(blocks, 0, "group"), 1, "core"), 2, "x")
    return blocks.transpose(3, 0, 2, 1, 4).reshape(n, -1)


def after(array, *earlier):
    return lax.optimization_barrier((array, *earlier))[0]


def ring_pieces(piece, axis, *gates):
    half = (piece.shape[0] + 31) // 32 * 16
    behind = shift(piece, axis, 1)
    ahead = shift(piece, axis, -1)
    top = shift(after(behind[:half], *gates), axis, 1)
    bottom = shift(after(ahead[half:], *gates), axis, -1)
    return [piece, ahead, top, bottom, behind]


def swapped(pieces):
    return [shift(p, "core", 1) for p in pieces]


def ring_starts(pieces, block, low):
    return [low, low + block, low + 2 * block, low + 2 * block + pieces[2].shape[0], low + 3 * block]


def feed_forward(rows, pieces, starts, hidden):
    tokens, columns = rows.shape[0], pieces[0].shape[1]
    width = sum(p.shape[0] for p in pieces)
    lanes = -(-hidden // 128) * 128
    count, groups = len(pieces), 4
    share = tokens // 4

    def kernel(rows_ref, *refs):
        activated_ref, outs = refs[count], refs[count + 1 : count + 9]
        whole, padded, sems = refs[count + 9 :]
        copies = [
            pltpu.make_async_copy(ref, whole.at[pl.ds(low, ref.shape[0]), :], sems.at[k])
            for k, (ref, low) in enumerate(zip(refs[:count], starts))
        ]
        for c in copies:
            c.start()
        padded[...] = jnp.zeros_like(padded)
        total = None
        for group in range(groups):
            for c in copies[group * count // groups : (group + 1) * count // groups]:
                c.wait()
            span = slice(group * width // groups, (group + 1) * width // groups)
            part = jnp.dot(rows_ref[:, span], whole[span, :], preferred_element_type=F32)
            total = part if total is None else total + part
        gate, up = total[:, hidden : 2 * hidden], total[:, 2 * hidden :]
        activated = (gate / (1.0 + jnp.exp(-gate)) * up).astype(BF16)
        activated_ref[...] = activated
        padded[:, :hidden] = activated
        for k in range(2):
            down = whole[k * width // 2 : (k + 1) * width // 2, :lanes]
            branch = lax.dot_general(
                padded[...], down, (((1,), (1,)), ((), ())), preferred_element_type=F32
            ).astype(BF16)
            for r in range(4):
                outs[4 * k + r][...] = branch[r * share : (r + 1) * share]

    block = jax.ShapeDtypeStruct((share, width // 2), BF16)
    out_shapes = [jax.ShapeDtypeStruct((tokens, hidden), BF16), *[block] * 8]
    activated, *blocks = pl.pallas_call(
        kernel,
        grid=(1,),
        in_specs=[
            pl.BlockSpec(rows.shape, lambda i: (0, 0)),
            *(pl.BlockSpec(memory_space=pltpu.HBM) for _ in pieces),
        ],
        out_specs=[pl.BlockSpec(o.shape, lambda i: (0, 0)) for o in out_shapes],
        out_shape=out_shapes,
        scratch_shapes=[
            pltpu.VMEM((width, columns), BF16),
            pltpu.VMEM((tokens, lanes), BF16),
            pltpu.SemaphoreType.DMA((count,)),
        ],
        compiler_params=pltpu.CompilerParams(vmem_limit_bytes=58 * 2**20),
    )(rows, *pieces)
    return activated, blocks[:4], blocks[4:]


def teacher_parts(rows, gain, weight, positions):
    each = rows.shape[0] // EP_LEN
    share = rows.shape[0] // 4
    sizes = (share, share, share // 2, share // 2, share)

    def kernel(positions_ref, rows_ref, gain_ref, weight_ref, *rest):
        outs, scaled = rest[:-1], rest[-1]
        for k in range(EP_LEN):
            low = pl.multiple_of(positions_ref[k] * each, each)
            wide = rows_ref[pl.ds(low, each), :].astype(F32)
            scaled[k * each : (k + 1) * each, :] = (wide * gain_ref[...]).astype(BF16)
        product = jnp.dot(scaled[...], weight_ref[...], preferred_element_type=F32).astype(BF16)
        low = 0
        for out, size in zip(outs, sizes):
            out[...] = product[low : low + size]
            low += size

    return pl.pallas_call(
        kernel,
        in_specs=[
            pl.BlockSpec(memory_space=pltpu.SMEM),
            *(pl.BlockSpec(memory_space=pltpu.VMEM) for _ in range(3)),
        ],
        out_specs=[pl.BlockSpec(memory_space=pltpu.VMEM) for _ in sizes],
        out_shape=[jax.ShapeDtypeStruct((size, weight.shape[1]), BF16) for size in sizes],
        scratch_shapes=[pltpu.VMEM(rows.shape, BF16)],
        compiler_params=pltpu.CompilerParams(vmem_limit_bytes=40 * 2**20),
    )(positions, rows, gain[None, :], weight)


def gather_z(rows):
    return jnp.concatenate([rows, *(exchange(rows, "z", k) for k in (1, 2, 3))], axis=0)


def gather_z_doubling(rows):
    pair = jnp.concatenate([rows, exchange(rows, "z", 1)], axis=0)
    return jnp.concatenate([pair, exchange(pair, "z", 2)], axis=0)


def added(parts, arrived):
    total = parts.astype(F32)
    for a in arrived:
        total = total + a.astype(F32)
    return total


def scatter_y(blocks):
    return added(blocks[0], [shift(blocks[k], "y", k) for k in (1, 2, 3)])


def scatter_z(parts):
    n = parts.shape[0] // 4
    return added(parts[:n], [exchange(parts[k * n : (k + 1) * n], "z", k) for k in (1, 2, 3)])


def scatter_z_halving(parts, *gates):
    n = parts.shape[0] // 4
    pair = added(parts[: 2 * n], [exchange(parts[2 * n :], "z", 2)])
    return added(pair[:n], [exchange(after(pair[n:].astype(BF16), *gates), "z", 1)])


def scatter_ring(own, first, top, bottom, third, axis, *gates):
    half = top.shape[0]
    top, bottom = shift(top, axis, 1), shift(bottom, axis, -1)
    up = jnp.concatenate([first[:half] + top, first[half:]], axis=0)
    down = jnp.concatenate([third[:half], third[half:] + bottom], axis=0)
    up, down = after(up, *gates), after(down, *gates)
    return added(own, [shift(up, axis, 1), shift(down, axis, -1)]), (top, bottom)


def two_parts(values):
    high = lax.reduce_precision(values, 8, 7)
    both = jnp.concatenate([high, values - high], axis=1).astype(BF16)
    return jnp.pad(both, ((0, 0), (0, 128 - both.shape[1])))


def pick(onehot, rows):
    return jnp.dot(onehot.astype(BF16), rows, preferred_element_type=F32).astype(BF16)


def to_owners(rows, owner_local, gate):
    owner = owner_local[:, 0]
    index = jnp.arange(owner.shape[0], dtype=jnp.int32)
    earlier = (owner[None, :] == owner[:, None]) & (index[None, :] < index[:, None])
    rank = jnp.sum(earlier.astype(jnp.int32), axis=1)
    g, x, c = (lax.axis_index(a) for a in OWNERS)
    to_c = (owner % 2 + c) % 2
    to_g = (owner // 8 + g) % 2
    to_x = (owner // 2 % 4 - x) % 4
    place = (to_g * 4 + to_x) * 2 + rank
    slots = jnp.arange(16, dtype=jnp.int32)[:, None]
    stay = pick((slots == place[None, :]) & (to_c[None, :] == 0), rows)
    leave = pick((slots == place[None, :]) & (to_c[None, :] == 1), rows)
    arrived = shift(leave, "core", 1)
    kept = jnp.concatenate([stay[:8], arrived[:8]], axis=0)
    sent = after(jnp.concatenate([stay[8:], arrived[8:]], axis=0), gate)
    both = jnp.concatenate([kept, shift(sent, "group", 1)], axis=0)
    place = jnp.arange(32, dtype=jnp.int32)
    by_x = pick((place // 2 % 4 * 4 + place // 8) * 2 + place % 2 == place[:, None], both)
    groups = [by_x[8 * k : 8 * (k + 1)] for k in range(4)]
    here = jnp.concatenate([groups[0], *(shift(groups[k], "x", k) for k in (1, 2, 3))], axis=0)
    source = jnp.arange(32, dtype=jnp.int32)
    k, sg, sc, r = source // 8, source // 4 % 2, source // 2 % 2, source % 2
    final = (((g + sg) % 2 * 4 + (x - k) % 4) * 2 + (c + sc) % 2) * 2 + r
    return pick(jnp.arange(32, dtype=jnp.int32)[:, None] == final[None, :], here)


def local(
    teacher_hidden,
    teacher_gain,
    project_weight,
    student_hidden,
    student_gain,
    gate_weight,
    up_weight,
    down_weight,
    owner_map,
    token_ids,
    token_counts,
    id_weight,
):
    episodes = token_counts.shape[0]
    hidden = gate_weight.shape[1]
    width = student_hidden.shape[1]
    block = width // 4
    position = lax.axis_index(TENSOR)
    tokens_all = EP_LEN * episodes * lax.axis_size(OWNERS)

    near = jnp.concatenate([down_weight.T, gate_weight, up_weight], axis=1)
    rows_each = near.shape[0]
    near_far = shift(near, "group", 1)
    near_own = ring_pieces(near, "x")
    near_first, near_last = (near_own[1], near_own[4]), (near_own[2], near_own[3])
    ahead = jnp.arange(EP_LEN, dtype=jnp.int32)
    positions = (lax.axis_index("z") ^ ahead % 4) * 4 + (lax.axis_index("y") + ahead // 4) % 4
    near_across = shift(near, "core", 1)
    rows = after(teacher_hidden, near_across, *near_first)
    parts = teacher_parts(rows, teacher_gain, project_weight, positions)
    near_relayed = [after(p, parts[0]) for p in near_last]
    near_other = [near_across, *swapped([near_own[1], *near_relayed, near_own[4]])]
    far_own = ring_pieces(after(near_far, *near_other), "x")
    far_first = (far_own[1], far_own[4])
    ahead, top, bottom, behind = far_own[1:]
    far_other = swapped([far_own[0], after(ahead, top, bottom), top, bottom, after(behind, top, bottom)])

    student_hidden, teacher_hidden = after(student_hidden, near), after(teacher_hidden, near)
    wide = student_hidden.astype(F32)
    rescale = lax.rsqrt(jnp.mean(wide * wide, axis=1, keepdims=True) + EPSILON)
    normed = (wide * rescale * student_gain[None, :]).astype(BF16)
    both_rows = relative_columns(jnp.concatenate([normed, student_hidden], axis=0))
    student = both_rows[episodes:].astype(F32)
    widened = teacher_hidden.astype(F32)
    squares = jnp.sum(widened * widened, axis=1).reshape(EP_LEN, episodes).T
    column = jnp.concatenate([both_rows[:episodes], two_parts(squares)], axis=1)
    column = gather_z_doubling(after(column, far_other[0], *near_other))
    gathered_pieces = ring_pieces(after(column, *far_first, far_other[0]), "y", far_other[1], far_other[4])
    gathered = jnp.concatenate(gathered_pieces, axis=0)
    totals = jnp.sum(gathered[:, width:].reshape(EP_LEN, episodes, -1).astype(F32), axis=0)
    totals = totals[:, :EP_LEN] + totals[:, EP_LEN : 2 * EP_LEN]
    totals = jnp.sum(jnp.where(jnp.arange(EP_LEN)[None, :] == position, totals, 0.0), axis=1)
    inverse = lax.rsqrt(totals / DT + EPSILON)

    total, _ = scatter_ring(*parts, "y")
    total = scatter_z_halving(after(total.astype(BF16), column))
    projected = (total * inverse[:, None]).astype(BF16)
    projected = relative_columns(projected).astype(F32)

    ids = jnp.arange(id_weight.shape[0], dtype=jnp.int32)
    looked = jnp.sum(jnp.where(token_ids[:, None] == ids[None, :], id_weight[None, :], 0.0), axis=1)
    weight = jnp.where(position < token_counts, looked, 0.0).astype(BF16).astype(F32)
    scale = 1.0 / math.sqrt(tokens_all)

    def starts(pieces, low):
        return ring_starts(pieces, rows_each, low) + ring_starts(pieces, rows_each, low + block)

    activated, near_branch, far_branch = feed_forward(
        after(gathered, total),
        near_own + near_other + far_own + far_other,
        starts(near_own, 0) + starts(far_own, 2 * block),
        hidden,
    )

    def gradient_half(far, branch_rows):
        columns = slice(far * 2 * block, (far + 1) * 2 * block)
        predicted = student[:, columns] + scatter_z(branch_rows)
        difference = predicted - projected[:, columns]
        return predicted, gather_z((weight[:, None] * difference * scale).astype(BF16))

    def owners_half(grad):
        mine, other = (
            jnp.einsum(
                "rc,rh->ch", grad[:, a : a + block], activated, preferred_element_type=F32
            ).astype(BF16)
            for a in (0, block)
        )
        both = mine + shift(other, "core", 1)
        quarter = block // 4
        own, first, second, third = (both[k * quarter : (k + 1) * quarter] for k in range(4))
        return own, first, second[: quarter // 2], second[quarter // 2 :], third

    far_rows = scatter_y(far_branch).astype(BF16)
    near_rows = scatter_y(near_branch).astype(BF16)
    far_predicted, far_column = gradient_half(1, far_rows)
    near_predicted, near_column = gradient_half(0, near_rows)
    far_ring, near_ring = ring_pieces(far_column, "y"), ring_pieces(near_column, "y")
    far_grad, near_grad = jnp.concatenate(far_ring, axis=0), jnp.concatenate(near_ring, axis=0)
    far_reduced, far_arrived = scatter_ring(*owners_half(far_grad), "x")
    far_reduced = far_reduced.astype(BF16)
    own, first, top, bottom, third = owners_half(near_grad)
    top, bottom = after(top, *far_arrived), after(bottom, *far_arrived)
    near_reduced, _ = scatter_ring(own, first, top, bottom, third, "x", far_reduced)
    down_grad = near_reduced + shift(far_reduced, "group", 1).astype(F32)

    predicted = [near_predicted, far_predicted]
    rows = jnp.concatenate([p.astype(BF16) for p in predicted], axis=1)
    student_out = to_owners(absolute_columns(rows), owner_map, far_ring[1])
    return (student_out[None, None], down_grad)


def solution(mesh):
    split = Mesh(mesh.devices.reshape(*AXES.values()), tuple(AXES))
    placed = (
        P(OWNERS, TENSOR),
        P(TENSOR),
        P(TENSOR, None),
        P((*OWNERS, *TENSOR), None),
        P(),
        P(OWNERS, TENSOR),
        P(OWNERS, TENSOR),
        P(TENSOR, OWNERS),
        P(OWNERS, None),
        P((*OWNERS, *TENSOR)),
        P(OWNERS),
        P(),
    )
    return jax.shard_map(
        local,
        mesh=split,
        in_specs=placed,
        out_specs=(P(OWNERS, TENSOR, None, None), P(OWNERS, TENSOR)),
        check_vma=False,
    )
```

```python
import math

import jax
import jax.numpy as jnp
from jax import lax
from jax.experimental import pallas as pl
from jax.experimental.pallas import tpu as pltpu
from jax.sharding import Mesh
from jax.sharding import PartitionSpec as P

DT = 8192
EP_LEN = 16
AXES = {"group": 2, "x": 4, "core": 2, "z": 4, "y": 4}
OWNERS = ("group", "x", "core")
TENSOR = ("z", "y")
EPSILON = 1e-06
F32 = jnp.float32
BF16 = jnp.bfloat16


def shift(array, axis, by):
    size = AXES[axis]
    return lax.ppermute(array, axis, [(i, (i + by) % size) for i in range(size)])


def rolled(array, axis, name):
    doubled = jnp.concatenate([array, array], axis=axis)
    return lax.dynamic_slice_in_dim(doubled, lax.axis_index(name), array.shape[axis], axis)


def unrolled(array, axis, name):
    size = array.shape[axis]
    doubled = jnp.concatenate([array, array], axis=axis)
    return lax.dynamic_slice_in_dim(doubled, size - lax.axis_index(name), size, axis)


def exchange(array, axis, bits):
    return lax.ppermute(array, axis, [(i, i ^ bits) for i in range(AXES[axis])])


def relative_columns(rows):
    n = rows.shape[0]
    blocks = rows.reshape(n, 2, 4, 2, -1).transpose(1, 3, 2, 0, 4)
    blocks = rolled(rolled(rolled(blocks, 0, "group"), 1, "core"), 2, "x")
    return blocks.transpose(3, 0, 1, 2, 4).reshape(n, -1)


def absolute_columns(rows):
    n = rows.shape[0]
    blocks = rows.reshape(n, 2, 2, 4, -1).transpose(1, 2, 3, 0, 4)
    blocks = unrolled(unrolled(unrolled(blocks, 0, "group"), 1, "core"), 2, "x")
    return blocks.transpose(3, 0, 2, 1, 4).reshape(n, -1)


def after(array, *earlier):
    return lax.optimization_barrier((array, *earlier))[0]


def ring_pieces(piece, axis, *gates):
    half = (piece.shape[0] + 31) // 32 * 16
    behind = shift(piece, axis, 1)
    ahead = shift(piece, axis, -1)
    top = shift(after(behind[:half], *gates), axis, 1)
    bottom = shift(after(ahead[half:], *gates), axis, -1)
    return [piece, ahead, top, bottom, behind]


def swapped(pieces):
    return [shift(p, "core", 1) for p in pieces]


def ring_starts(pieces, block, low):
    return [low, low + block, low + 2 * block, low + 2 * block + pieces[2].shape[0], low + 3 * block]


def feed_forward(rows, pieces, starts, hidden):
    tokens, columns = rows.shape[0], pieces[0].shape[1]
    width = sum(p.shape[0] for p in pieces)
    lanes = -(-hidden // 128) * 128
    count, groups = len(pieces), 4
    share = tokens // 4

    def kernel(rows_ref, *refs):
        activated_ref, outs = refs[count], refs[count + 1 : count + 9]
        whole, padded, sems = refs[count + 9 :]
        copies = [
            pltpu.make_async_copy(ref, whole.at[pl.ds(low, ref.shape[0]), :], sems.at[k])
            for k, (ref, low) in enumerate(zip(refs[:count], starts))
        ]
        for c in copies:
            c.start()
        padded[...] = jnp.zeros_like(padded)
        total = None
        for group in range(groups):
            for c in copies[group * count // groups : (group + 1) * count // groups]:
                c.wait()
            span = slice(group * width // groups, (group + 1) * width // groups)
            part = jnp.dot(rows_ref[:, span], whole[span, :], preferred_element_type=F32)
            total = part if total is None else total + part
        gate, up = total[:, hidden : 2 * hidden], total[:, 2 * hidden :]
        activated = (gate / (1.0 + jnp.exp(-gate)) * up).astype(BF16)
        activated_ref[...] = activated
        padded[:, :hidden] = activated
        for k in range(2):
            down = whole[k * width // 2 : (k + 1) * width // 2, :lanes]
            branch = lax.dot_general(
                padded[...], down, (((1,), (1,)), ((), ())), preferred_element_type=F32
            ).astype(BF16)
            for r in range(4):
                outs[4 * k + r][...] = branch[r * share : (r + 1) * share]

    block = jax.ShapeDtypeStruct((share, width // 2), BF16)
    out_shapes = [jax.ShapeDtypeStruct((tokens, hidden), BF16), *[block] * 8]
    activated, *blocks = pl.pallas_call(
        kernel,
        grid=(1,),
        in_specs=[
            pl.BlockSpec(rows.shape, lambda i: (0, 0)),
            *(pl.BlockSpec(memory_space=pltpu.HBM) for _ in pieces),
        ],
        out_specs=[pl.BlockSpec(o.shape, lambda i: (0, 0)) for o in out_shapes],
        out_shape=out_shapes,
        scratch_shapes=[
            pltpu.VMEM((width, columns), BF16),
            pltpu.VMEM((tokens, lanes), BF16),
            pltpu.SemaphoreType.DMA((count,)),
        ],
        compiler_params=pltpu.CompilerParams(vmem_limit_bytes=58 * 2**20),
    )(rows, *pieces)
    return activated, blocks[:4], blocks[4:]


def teacher_parts(rows, gain, weight, positions):
    each = rows.shape[0] // EP_LEN
    share = rows.shape[0] // 4
    sizes = (share, share, share // 2, share // 2, share)

    def kernel(positions_ref, rows_ref, gain_ref, weight_ref, *rest):
        outs, scaled = rest[:-1], rest[-1]
        for k in range(EP_LEN):
            low = pl.multiple_of(positions_ref[k] * each, each)
            wide = rows_ref[pl.ds(low, each), :].astype(F32)
            scaled[k * each : (k + 1) * each, :] = (wide * gain_ref[...]).astype(BF16)
        product = jnp.dot(scaled[...], weight_ref[...], preferred_element_type=F32).astype(BF16)
        low = 0
        for out, size in zip(outs, sizes):
            out[...] = product[low : low + size]
            low += size

    return pl.pallas_call(
        kernel,
        in_specs=[
            pl.BlockSpec(memory_space=pltpu.SMEM),
            *(pl.BlockSpec(memory_space=pltpu.VMEM) for _ in range(3)),
        ],
        out_specs=[pl.BlockSpec(memory_space=pltpu.VMEM) for _ in sizes],
        out_shape=[jax.ShapeDtypeStruct((size, weight.shape[1]), BF16) for size in sizes],
        scratch_shapes=[pltpu.VMEM(rows.shape, BF16)],
        compiler_params=pltpu.CompilerParams(vmem_limit_bytes=40 * 2**20),
    )(positions, rows, gain[None, :], weight)


def gather_z(rows):
    return jnp.concatenate([rows, *(exchange(rows, "z", k) for k in (1, 2, 3))], axis=0)


def added(parts, arrived):
    total = parts.astype(F32)
    for a in arrived:
        total = total + a.astype(F32)
    return total


def scatter_y(blocks):
    return added(blocks[0], [shift(blocks[k], "y", k) for k in (1, 2, 3)])


def scatter_z(parts):
    n = parts.shape[0] // 4
    return added(parts[:n], [exchange(parts[k * n : (k + 1) * n], "z", k) for k in (1, 2, 3)])


def scatter_z_halving(parts, *gates):
    n = parts.shape[0] // 4
    pair = added(parts[: 2 * n], [exchange(parts[2 * n :], "z", 2)])
    return added(pair[:n], [exchange(after(pair[n:].astype(BF16), *gates), "z", 1)])


def scatter_ring(own, first, top, bottom, third, axis, *gates):
    half = top.shape[0]
    top, bottom = shift(top, axis, 1), shift(bottom, axis, -1)
    up = jnp.concatenate([first[:half] + top, first[half:]], axis=0)
    down = jnp.concatenate([third[:half], third[half:] + bottom], axis=0)
    up, down = after(up, *gates), after(down, *gates)
    return added(own, [shift(up, axis, 1), shift(down, axis, -1)]), (top, bottom)


def two_parts(values):
    high = lax.reduce_precision(values, 8, 7)
    both = jnp.concatenate([high, values - high], axis=1).astype(BF16)
    return jnp.pad(both, ((0, 0), (0, 128 - both.shape[1])))


def pick(onehot, rows):
    return jnp.dot(onehot.astype(BF16), rows, preferred_element_type=F32).astype(BF16)


def to_owners(rows, owner_local, gate):
    owner = owner_local[:, 0]
    index = jnp.arange(owner.shape[0], dtype=jnp.int32)
    earlier = (owner[None, :] == owner[:, None]) & (index[None, :] < index[:, None])
    rank = jnp.sum(earlier.astype(jnp.int32), axis=1)
    g, x, c = (lax.axis_index(a) for a in OWNERS)
    to_c = (owner % 2 + c) % 2
    to_g = (owner // 8 + g) % 2
    to_x = (owner // 2 % 4 - x) % 4
    place = (to_g * 4 + to_x) * 2 + rank
    slots = jnp.arange(16, dtype=jnp.int32)[:, None]
    stay = pick((slots == place[None, :]) & (to_c[None, :] == 0), rows)
    leave = pick((slots == place[None, :]) & (to_c[None, :] == 1), rows)
    arrived = shift(leave, "core", 1)
    kept = jnp.concatenate([stay[:8], arrived[:8]], axis=0)
    sent = after(jnp.concatenate([stay[8:], arrived[8:]], axis=0), gate)
    both = jnp.concatenate([kept, shift(sent, "group", 1)], axis=0)
    place = jnp.arange(32, dtype=jnp.int32)
    by_x = pick((place // 2 % 4 * 4 + place // 8) * 2 + place % 2 == place[:, None], both)
    groups = [by_x[8 * k : 8 * (k + 1)] for k in range(4)]
    here = jnp.concatenate([groups[0], *(shift(groups[k], "x", k) for k in (1, 2, 3))], axis=0)
    source = jnp.arange(32, dtype=jnp.int32)
    k, sg, sc, r = source // 8, source // 4 % 2, source // 2 % 2, source % 2
    final = (((g + sg) % 2 * 4 + (x - k) % 4) * 2 + (c + sc) % 2) * 2 + r
    return pick(jnp.arange(32, dtype=jnp.int32)[:, None] == final[None, :], here)


def local(
    teacher_hidden,
    teacher_gain,
    project_weight,
    student_hidden,
    student_gain,
    gate_weight,
    up_weight,
    down_weight,
    owner_map,
    token_ids,
    token_counts,
    id_weight,
):
    episodes = token_counts.shape[0]
    hidden = gate_weight.shape[1]
    width = student_hidden.shape[1]
    block = width // 4
    position = lax.axis_index(TENSOR)
    tokens_all = EP_LEN * episodes * lax.axis_size(OWNERS)

    near = jnp.concatenate([down_weight.T, gate_weight, up_weight], axis=1)
    rows_each = near.shape[0]
    near_far = shift(near, "group", 1)
    near_own = ring_pieces(near, "x")
    near_first, near_last = (near_own[1], near_own[4]), (near_own[2], near_own[3])
    ahead = jnp.arange(EP_LEN, dtype=jnp.int32)
    positions = (lax.axis_index("z") ^ ahead % 4) * 4 + (lax.axis_index("y") + ahead // 4) % 4
    near_across = shift(near, "core", 1)
    rows = after(teacher_hidden, near_across, *near_first)
    parts = teacher_parts(rows, teacher_gain, project_weight, positions)
    near_relayed = [after(p, parts[0]) for p in near_last]
    near_other = [near_across, *swapped([near_own[1], *near_relayed, near_own[4]])]
    student_hidden, teacher_hidden = after(student_hidden, near), after(teacher_hidden, near)
    wide = student_hidden.astype(F32)
    rescale = lax.rsqrt(jnp.mean(wide * wide, axis=1, keepdims=True) + EPSILON)
    normed = (wide * rescale * student_gain[None, :]).astype(BF16)
    both_rows = relative_columns(jnp.concatenate([normed, student_hidden], axis=0))
    student = both_rows[episodes:].astype(F32)
    widened = teacher_hidden.astype(F32)
    squares = jnp.sum(widened * widened, axis=1).reshape(EP_LEN, episodes).T
    column = jnp.concatenate([both_rows[:episodes], two_parts(squares)], axis=1)
    column = after(column, near_far, *near_other)
    pair = jnp.concatenate([column, exchange(column, "z", 1)], axis=0)
    column = jnp.concatenate([pair, exchange(pair, "z", 2)], axis=0)
    far_own = ring_pieces(after(near_far, pair), "x")
    far_first = (far_own[1], far_own[4])
    ahead, top, bottom, behind = far_own[1:]
    far_other = swapped([far_own[0], after(ahead, top, bottom), top, bottom, after(behind, top, bottom)])
    gathered_pieces = ring_pieces(after(column, *far_first, far_other[0]), "y", far_other[1], far_other[4])
    gathered = jnp.concatenate(gathered_pieces, axis=0)
    totals = jnp.sum(gathered[:, width:].reshape(EP_LEN, episodes, -1).astype(F32), axis=0)
    totals = totals[:, :EP_LEN] + totals[:, EP_LEN : 2 * EP_LEN]
    totals = jnp.sum(jnp.where(jnp.arange(EP_LEN)[None, :] == position, totals, 0.0), axis=1)
    inverse = lax.rsqrt(totals / DT + EPSILON)

    total, _ = scatter_ring(*parts, "y")
    total = scatter_z_halving(after(total.astype(BF16), column))
    projected = (total * inverse[:, None]).astype(BF16)
    projected = relative_columns(projected).astype(F32)

    ids = jnp.arange(id_weight.shape[0], dtype=jnp.int32)
    looked = jnp.sum(jnp.where(token_ids[:, None] == ids[None, :], id_weight[None, :], 0.0), axis=1)
    weight = jnp.where(position < token_counts, looked, 0.0).astype(BF16).astype(F32)
    scale = 1.0 / math.sqrt(tokens_all)

    def starts(pieces, low):
        return ring_starts(pieces, rows_each, low) + ring_starts(pieces, rows_each, low + block)

    activated, near_branch, far_branch = feed_forward(
        after(gathered, total),
        near_own + near_other + far_own + far_other,
        starts(near_own, 0) + starts(far_own, 2 * block),
        hidden,
    )

    def gradient_half(far, branch_rows):
        columns = slice(far * 2 * block, (far + 1) * 2 * block)
        predicted = student[:, columns] + scatter_z(branch_rows)
        difference = predicted - projected[:, columns]
        return predicted, gather_z((weight[:, None] * difference * scale).astype(BF16))

    def owners_half(grad):
        mine, other = (
            jnp.einsum(
                "rc,rh->ch", grad[:, a : a + block], activated, preferred_element_type=F32
            ).astype(BF16)
            for a in (0, block)
        )
        both = mine + shift(other, "core", 1)
        quarter = block // 4
        own, first, second, third = (both[k * quarter : (k + 1) * quarter] for k in range(4))
        return own, first, second[: quarter // 2], second[quarter // 2 :], third

    far_rows = scatter_y(far_branch).astype(BF16)
    near_rows = scatter_y(near_branch).astype(BF16)
    far_predicted, far_column = gradient_half(1, far_rows)
    near_predicted, near_column = gradient_half(0, near_rows)
    far_ring, near_ring = ring_pieces(far_column, "y"), ring_pieces(near_column, "y")
    far_grad, near_grad = jnp.concatenate(far_ring, axis=0), jnp.concatenate(near_ring, axis=0)
    far_reduced, far_arrived = scatter_ring(*owners_half(far_grad), "x")
    far_reduced = far_reduced.astype(BF16)
    own, first, top, bottom, third = owners_half(near_grad)
    top, bottom = after(top, *far_arrived), after(bottom, *far_arrived)
    near_reduced, _ = scatter_ring(own, first, top, bottom, third, "x", far_reduced)
    down_grad = near_reduced + shift(far_reduced, "group", 1).astype(F32)

    predicted = [near_predicted, far_predicted]
    rows = jnp.concatenate([p.astype(BF16) for p in predicted], axis=1)
    student_out = to_owners(absolute_columns(rows), owner_map, far_arrived[0])
    return (student_out[None, None], down_grad)


def solution(mesh):
    split = Mesh(mesh.devices.reshape(*AXES.values()), tuple(AXES))
    placed = (
        P(OWNERS, TENSOR),
        P(TENSOR),
        P(TENSOR, None),
        P((*OWNERS, *TENSOR), None),
        P(),
        P(OWNERS, TENSOR),
        P(OWNERS, TENSOR),
        P(TENSOR, OWNERS),
        P(OWNERS, None),
        P((*OWNERS, *TENSOR)),
        P(OWNERS),
        P(),
    )
    return jax.shard_map(
        local,
        mesh=split,
        in_specs=placed,
        out_specs=(P(OWNERS, TENSOR, None, None), P(OWNERS, TENSOR)),
        check_vma=False,
    )
```

```python
import math

import jax
import jax.numpy as jnp
from jax import lax
from jax.experimental import pallas as pl
from jax.experimental.pallas import tpu as pltpu
from jax.sharding import Mesh
from jax.sharding import PartitionSpec as P

DT = 8192
EP_LEN = 16
AXES = {"group": 2, "x": 4, "core": 2, "z": 4, "y": 4}
OWNERS = ("group", "x", "core")
TENSOR = ("z", "y")
EPSILON = 1e-06
F32 = jnp.float32
BF16 = jnp.bfloat16


def shift(array, axis, by):
    size = AXES[axis]
    return lax.ppermute(array, axis, [(i, (i + by) % size) for i in range(size)])


def rolled(array, axis, name):
    doubled = jnp.concatenate([array, array], axis=axis)
    return lax.dynamic_slice_in_dim(doubled, lax.axis_index(name), array.shape[axis], axis)


def unrolled(array, axis, name):
    size = array.shape[axis]
    doubled = jnp.concatenate([array, array], axis=axis)
    return lax.dynamic_slice_in_dim(doubled, size - lax.axis_index(name), size, axis)


def exchange(array, axis, bits):
    return lax.ppermute(array, axis, [(i, i ^ bits) for i in range(AXES[axis])])


def relative_columns(rows):
    n = rows.shape[0]
    blocks = rows.reshape(n, 2, 4, 2, -1).transpose(1, 3, 2, 0, 4)
    blocks = rolled(rolled(rolled(blocks, 0, "group"), 1, "core"), 2, "x")
    return blocks.transpose(3, 0, 1, 2, 4).reshape(n, -1)


def absolute_columns(rows):
    n = rows.shape[0]
    blocks = rows.reshape(n, 2, 2, 4, -1).transpose(1, 2, 3, 0, 4)
    blocks = unrolled(unrolled(unrolled(blocks, 0, "group"), 1, "core"), 2, "x")
    return blocks.transpose(3, 0, 2, 1, 4).reshape(n, -1)


def after(array, *earlier):
    return lax.optimization_barrier((array, *earlier))[0]


def ring_pieces(piece, axis, *gates):
    half = (piece.shape[0] + 31) // 32 * 16
    behind = shift(piece, axis, 1)
    ahead = shift(piece, axis, -1)
    top = shift(after(behind[:half], *gates), axis, 1)
    bottom = shift(after(ahead[half:], *gates), axis, -1)
    return [piece, ahead, top, bottom, behind]


def swapped(pieces):
    return [shift(p, "core", 1) for p in pieces]


def ring_starts(pieces, block, low):
    return [low, low + block, low + 2 * block, low + 2 * block + pieces[2].shape[0], low + 3 * block]


def feed_forward(rows, pieces, starts, hidden):
    tokens, columns = rows.shape[0], pieces[0].shape[1]
    width = sum(p.shape[0] for p in pieces)
    lanes = -(-hidden // 128) * 128
    count, groups = len(pieces), 4
    share = tokens // 4

    def kernel(rows_ref, *refs):
        activated_ref, outs = refs[count], refs[count + 1 : count + 9]
        whole, padded, sems = refs[count + 9 :]
        copies = [
            pltpu.make_async_copy(ref, whole.at[pl.ds(low, ref.shape[0]), :], sems.at[k])
            for k, (ref, low) in enumerate(zip(refs[:count], starts))
        ]
        for c in copies:
            c.start()
        padded[...] = jnp.zeros_like(padded)
        total = None
        for group in range(groups):
            for c in copies[group * count // groups : (group + 1) * count // groups]:
                c.wait()
            span = slice(group * width // groups, (group + 1) * width // groups)
            part = jnp.dot(rows_ref[:, span], whole[span, :], preferred_element_type=F32)
            total = part if total is None else total + part
        gate, up = total[:, hidden : 2 * hidden], total[:, 2 * hidden :]
        activated = (gate / (1.0 + jnp.exp(-gate)) * up).astype(BF16)
        activated_ref[...] = activated
        padded[:, :hidden] = activated
        for k in range(2):
            down = whole[k * width // 2 : (k + 1) * width // 2, :lanes]
            branch = lax.dot_general(
                padded[...], down, (((1,), (1,)), ((), ())), preferred_element_type=F32
            ).astype(BF16)
            for r in range(4):
                outs[4 * k + r][...] = branch[r * share : (r + 1) * share]

    block = jax.ShapeDtypeStruct((share, width // 2), BF16)
    out_shapes = [jax.ShapeDtypeStruct((tokens, hidden), BF16), *[block] * 8]
    activated, *blocks = pl.pallas_call(
        kernel,
        grid=(1,),
        in_specs=[
            pl.BlockSpec(rows.shape, lambda i: (0, 0)),
            *(pl.BlockSpec(memory_space=pltpu.HBM) for _ in pieces),
        ],
        out_specs=[pl.BlockSpec(o.shape, lambda i: (0, 0)) for o in out_shapes],
        out_shape=out_shapes,
        scratch_shapes=[
            pltpu.VMEM((width, columns), BF16),
            pltpu.VMEM((tokens, lanes), BF16),
            pltpu.SemaphoreType.DMA((count,)),
        ],
        compiler_params=pltpu.CompilerParams(vmem_limit_bytes=58 * 2**20),
    )(rows, *pieces)
    return activated, blocks[:4], blocks[4:]


def teacher_parts(rows, gain, weight, positions):
    each = rows.shape[0] // EP_LEN
    share = rows.shape[0] // 4
    sizes = (share, share, share // 2, share // 2, share)

    def kernel(positions_ref, rows_ref, gain_ref, weight_ref, *rest):
        outs, scaled = rest[:-1], rest[-1]
        for k in range(EP_LEN):
            low = pl.multiple_of(positions_ref[k] * each, each)
            wide = rows_ref[pl.ds(low, each), :].astype(F32)
            scaled[k * each : (k + 1) * each, :] = (wide * gain_ref[...]).astype(BF16)
        product = jnp.dot(scaled[...], weight_ref[...], preferred_element_type=F32).astype(BF16)
        low = 0
        for out, size in zip(outs, sizes):
            out[...] = product[low : low + size]
            low += size

    return pl.pallas_call(
        kernel,
        in_specs=[
            pl.BlockSpec(memory_space=pltpu.SMEM),
            *(pl.BlockSpec(memory_space=pltpu.VMEM) for _ in range(3)),
        ],
        out_specs=[pl.BlockSpec(memory_space=pltpu.VMEM) for _ in sizes],
        out_shape=[jax.ShapeDtypeStruct((size, weight.shape[1]), BF16) for size in sizes],
        scratch_shapes=[pltpu.VMEM(rows.shape, BF16)],
        compiler_params=pltpu.CompilerParams(vmem_limit_bytes=40 * 2**20),
    )(positions, rows, gain[None, :], weight)


def gather_z(rows):
    return jnp.concatenate([rows, *(exchange(rows, "z", k) for k in (1, 2, 3))], axis=0)


def added(parts, arrived):
    total = parts.astype(F32)
    for a in arrived:
        total = total + a.astype(F32)
    return total


def scatter_y(blocks):
    return added(blocks[0], [shift(blocks[k], "y", k) for k in (1, 2, 3)])


def scatter_z(parts):
    n = parts.shape[0] // 4
    return added(parts[:n], [exchange(parts[k * n : (k + 1) * n], "z", k) for k in (1, 2, 3)])


def scatter_z_halving(parts, *gates):
    n = parts.shape[0] // 4
    pair = added(parts[: 2 * n], [exchange(parts[2 * n :], "z", 2)])
    return added(pair[:n], [exchange(after(pair[n:].astype(BF16), *gates), "z", 1)])


def scatter_ring(own, first, top, bottom, third, axis, *gates):
    half = top.shape[0]
    top, bottom = shift(top, axis, 1), shift(bottom, axis, -1)
    up = jnp.concatenate([first[:half] + top, first[half:]], axis=0)
    down = jnp.concatenate([third[:half], third[half:] + bottom], axis=0)
    up, down = after(up, *gates), after(down, *gates)
    return added(own, [shift(up, axis, 1), shift(down, axis, -1)]), (top, bottom)


def two_parts(values):
    high = lax.reduce_precision(values, 8, 7)
    both = jnp.concatenate([high, values - high], axis=1).astype(BF16)
    return jnp.pad(both, ((0, 0), (0, 128 - both.shape[1])))


def pick(onehot, rows):
    return jnp.dot(onehot.astype(BF16), rows, preferred_element_type=F32).astype(BF16)


def to_owners(rows, owner_local, gate):
    owner = owner_local[:, 0]
    index = jnp.arange(owner.shape[0], dtype=jnp.int32)
    earlier = (owner[None, :] == owner[:, None]) & (index[None, :] < index[:, None])
    rank = jnp.sum(earlier.astype(jnp.int32), axis=1)
    g, x, c = (lax.axis_index(a) for a in OWNERS)
    to_c = (owner % 2 + c) % 2
    to_g = (owner // 8 + g) % 2
    to_x = (owner // 2 % 4 - x) % 4
    place = (to_g * 4 + to_x) * 2 + rank
    slots = jnp.arange(16, dtype=jnp.int32)[:, None]
    stay = pick((slots == place[None, :]) & (to_c[None, :] == 0), rows)
    leave = pick((slots == place[None, :]) & (to_c[None, :] == 1), rows)
    arrived = shift(leave, "core", 1)
    kept = jnp.concatenate([stay[:8], arrived[:8]], axis=0)
    sent = after(jnp.concatenate([stay[8:], arrived[8:]], axis=0), gate)
    both = jnp.concatenate([kept, shift(sent, "group", 1)], axis=0)
    place = jnp.arange(32, dtype=jnp.int32)
    by_x = pick((place // 2 % 4 * 4 + place // 8) * 2 + place % 2 == place[:, None], both)
    groups = [by_x[8 * k : 8 * (k + 1)] for k in range(4)]
    here = jnp.concatenate([groups[0], *(shift(groups[k], "x", k) for k in (1, 2, 3))], axis=0)
    source = jnp.arange(32, dtype=jnp.int32)
    k, sg, sc, r = source // 8, source // 4 % 2, source // 2 % 2, source % 2
    final = (((g + sg) % 2 * 4 + (x - k) % 4) * 2 + (c + sc) % 2) * 2 + r
    return pick(jnp.arange(32, dtype=jnp.int32)[:, None] == final[None, :], here)


def local(
    teacher_hidden,
    teacher_gain,
    project_weight,
    student_hidden,
    student_gain,
    gate_weight,
    up_weight,
    down_weight,
    owner_map,
    token_ids,
    token_counts,
    id_weight,
):
    episodes = token_counts.shape[0]
    hidden = gate_weight.shape[1]
    width = student_hidden.shape[1]
    block = width // 4
    position = lax.axis_index(TENSOR)
    tokens_all = EP_LEN * episodes * lax.axis_size(OWNERS)

    near = jnp.concatenate([down_weight.T, gate_weight, up_weight], axis=1)
    rows_each = near.shape[0]
    near_far = shift(near, "group", 1)
    ahead = jnp.arange(EP_LEN, dtype=jnp.int32)
    positions = (lax.axis_index("z") ^ ahead % 4) * 4 + (lax.axis_index("y") + ahead // 4) % 4
    near_across = shift(near, "core", 1)
    rows = after(teacher_hidden, near_across)
    parts = teacher_parts(rows, teacher_gain, project_weight, positions)
    near_own = ring_pieces(near, "x", parts[0])
    near_first, near_last = (near_own[1], near_own[4]), (near_own[2], near_own[3])
    parts = [after(p, *near_first) for p in parts]
    near_other = [near_across, *swapped(near_own[1:])]
    student_hidden, teacher_hidden = after(student_hidden, near), after(teacher_hidden, near)
    wide = student_hidden.astype(F32)
    rescale = lax.rsqrt(jnp.mean(wide * wide, axis=1, keepdims=True) + EPSILON)
    normed = (wide * rescale * student_gain[None, :]).astype(BF16)
    both_rows = relative_columns(jnp.concatenate([normed, student_hidden], axis=0))
    student = both_rows[episodes:].astype(F32)
    widened = teacher_hidden.astype(F32)
    squares = jnp.sum(widened * widened, axis=1).reshape(EP_LEN, episodes).T
    column = jnp.concatenate([both_rows[:episodes], two_parts(squares)], axis=1)
    column = after(column, near_far, *near_other)
    pair = jnp.concatenate([column, exchange(column, "z", 1)], axis=0)
    column = jnp.concatenate([pair, exchange(pair, "z", 2)], axis=0)
    far_own = ring_pieces(after(near_far, pair), "x")
    far_first = (far_own[1], far_own[4])
    ahead, top, bottom, behind = far_own[1:]
    far_other = swapped([far_own[0], after(ahead, top, bottom), top, bottom, after(behind, top, bottom)])
    gathered_pieces = ring_pieces(after(column, *far_first, far_other[0]), "y", far_other[1], far_other[4])
    gathered = jnp.concatenate(gathered_pieces, axis=0)
    totals = jnp.sum(gathered[:, width:].reshape(EP_LEN, episodes, -1).astype(F32), axis=0)
    totals = totals[:, :EP_LEN] + totals[:, EP_LEN : 2 * EP_LEN]
    totals = jnp.sum(jnp.where(jnp.arange(EP_LEN)[None, :] == position, totals, 0.0), axis=1)
    inverse = lax.rsqrt(totals / DT + EPSILON)

    total, _ = scatter_ring(*parts, "y")
    total = scatter_z_halving(after(total.astype(BF16), column))
    projected = (total * inverse[:, None]).astype(BF16)
    projected = relative_columns(projected).astype(F32)

    ids = jnp.arange(id_weight.shape[0], dtype=jnp.int32)
    looked = jnp.sum(jnp.where(token_ids[:, None] == ids[None, :], id_weight[None, :], 0.0), axis=1)
    weight = jnp.where(position < token_counts, looked, 0.0).astype(BF16).astype(F32)
    scale = 1.0 / math.sqrt(tokens_all)

    def starts(pieces, low):
        return ring_starts(pieces, rows_each, low) + ring_starts(pieces, rows_each, low + block)

    activated, near_branch, far_branch = feed_forward(
        after(gathered, total),
        near_own + near_other + far_own + far_other,
        starts(near_own, 0) + starts(far_own, 2 * block),
        hidden,
    )

    def gradient_half(far, branch_rows):
        columns = slice(far * 2 * block, (far + 1) * 2 * block)
        predicted = student[:, columns] + scatter_z(branch_rows)
        difference = predicted - projected[:, columns]
        return predicted, gather_z((weight[:, None] * difference * scale).astype(BF16))

    def owners_half(grad):
        mine, other = (
            jnp.einsum(
                "rc,rh->ch", grad[:, a : a + block], activated, preferred_element_type=F32
            ).astype(BF16)
            for a in (0, block)
        )
        both = mine + shift(other, "core", 1)
        quarter = block // 4
        own, first, second, third = (both[k * quarter : (k + 1) * quarter] for k in range(4))
        return own, first, second[: quarter // 2], second[quarter // 2 :], third

    far_rows = scatter_y(far_branch).astype(BF16)
    near_rows = scatter_y(near_branch).astype(BF16)
    far_predicted, far_column = gradient_half(1, far_rows)
    near_predicted, near_column = gradient_half(0, near_rows)
    far_ring, near_ring = ring_pieces(far_column, "y"), ring_pieces(near_column, "y")
    far_grad, near_grad = jnp.concatenate(far_ring, axis=0), jnp.concatenate(near_ring, axis=0)
    far_reduced, far_arrived = scatter_ring(*owners_half(far_grad), "x")
    far_reduced = far_reduced.astype(BF16)
    own, first, top, bottom, third = owners_half(near_grad)
    top, bottom = after(top, *far_arrived), after(bottom, *far_arrived)
    near_reduced, _ = scatter_ring(own, first, top, bottom, third, "x", far_reduced)
    down_grad = near_reduced + shift(far_reduced, "group", 1).astype(F32)

    predicted = [near_predicted, far_predicted]
    rows = jnp.concatenate([p.astype(BF16) for p in predicted], axis=1)
    student_out = to_owners(absolute_columns(rows), owner_map, far_arrived[0])
    return (student_out[None, None], down_grad)


def solution(mesh):
    split = Mesh(mesh.devices.reshape(*AXES.values()), tuple(AXES))
    placed = (
        P(OWNERS, TENSOR),
        P(TENSOR),
        P(TENSOR, None),
        P((*OWNERS, *TENSOR), None),
        P(),
        P(OWNERS, TENSOR),
        P(OWNERS, TENSOR),
        P(TENSOR, OWNERS),
        P(OWNERS, None),
        P((*OWNERS, *TENSOR)),
        P(OWNERS),
        P(),
    )
    return jax.shard_map(
        local,
        mesh=split,
        in_specs=placed,
        out_specs=(P(OWNERS, TENSOR, None, None), P(OWNERS, TENSOR)),
        check_vma=False,
    )
```

```python
import math

import jax
import jax.numpy as jnp
from jax import lax
from jax.experimental import pallas as pl
from jax.experimental.pallas import tpu as pltpu
from jax.sharding import Mesh
from jax.sharding import PartitionSpec as P

DT = 8192
EP_LEN = 16
AXES = {"group": 2, "x": 4, "core": 2, "z": 4, "y": 4}
OWNERS = ("group", "x", "core")
TENSOR = ("z", "y")
EPSILON = 1e-06
F32 = jnp.float32
BF16 = jnp.bfloat16


def shift(array, axis, by):
    size = AXES[axis]
    return lax.ppermute(array, axis, [(i, (i + by) % size) for i in range(size)])


def rolled(array, axis, name):
    doubled = jnp.concatenate([array, array], axis=axis)
    return lax.dynamic_slice_in_dim(doubled, lax.axis_index(name), array.shape[axis], axis)


def unrolled(array, axis, name):
    size = array.shape[axis]
    doubled = jnp.concatenate([array, array], axis=axis)
    return lax.dynamic_slice_in_dim(doubled, size - lax.axis_index(name), size, axis)


def exchange(array, axis, bits):
    return lax.ppermute(array, axis, [(i, i ^ bits) for i in range(AXES[axis])])


def relative_columns(rows):
    n = rows.shape[0]
    blocks = rows.reshape(n, 2, 4, 2, -1).transpose(1, 3, 2, 0, 4)
    blocks = rolled(rolled(rolled(blocks, 0, "group"), 1, "core"), 2, "x")
    return blocks.transpose(3, 0, 1, 2, 4).reshape(n, -1)


def absolute_columns(rows):
    n = rows.shape[0]
    blocks = rows.reshape(n, 2, 2, 4, -1).transpose(1, 2, 3, 0, 4)
    blocks = unrolled(unrolled(unrolled(blocks, 0, "group"), 1, "core"), 2, "x")
    return blocks.transpose(3, 0, 2, 1, 4).reshape(n, -1)


def after(array, *earlier):
    return lax.optimization_barrier((array, *earlier))[0]


def ring_pieces(piece, axis, *gates):
    half = (piece.shape[0] + 31) // 32 * 16
    behind = shift(piece, axis, 1)
    ahead = shift(piece, axis, -1)
    top = shift(after(behind[:half], *gates), axis, 1)
    bottom = shift(after(ahead[half:], *gates), axis, -1)
    return [piece, ahead, top, bottom, behind]


def swapped(pieces):
    return [shift(p, "core", 1) for p in pieces]


def ring_starts(pieces, block, low):
    return [low, low + block, low + 2 * block, low + 2 * block + pieces[2].shape[0], low + 3 * block]


def feed_forward(rows, pieces, starts, hidden):
    tokens, columns = rows.shape[0], pieces[0].shape[1]
    width = sum(p.shape[0] for p in pieces)
    lanes = -(-hidden // 128) * 128
    count, groups = len(pieces), 4
    share = tokens // 4

    def kernel(rows_ref, *refs):
        activated_ref, outs = refs[count], refs[count + 1 : count + 9]
        whole, padded, sems = refs[count + 9 :]
        copies = [
            pltpu.make_async_copy(ref, whole.at[pl.ds(low, ref.shape[0]), :], sems.at[k])
            for k, (ref, low) in enumerate(zip(refs[:count], starts))
        ]
        for c in copies:
            c.start()
        padded[...] = jnp.zeros_like(padded)
        total = None
        for group in range(groups):
            for c in copies[group * count // groups : (group + 1) * count // groups]:
                c.wait()
            span = slice(group * width // groups, (group + 1) * width // groups)
            part = jnp.dot(rows_ref[:, span], whole[span, :], preferred_element_type=F32)
            total = part if total is None else total + part
        gate, up = total[:, hidden : 2 * hidden], total[:, 2 * hidden :]
        activated = (gate / (1.0 + jnp.exp(-gate)) * up).astype(BF16)
        activated_ref[...] = activated
        padded[:, :hidden] = activated
        for k in range(2):
            down = whole[k * width // 2 : (k + 1) * width // 2, :lanes]
            branch = lax.dot_general(
                padded[...], down, (((1,), (1,)), ((), ())), preferred_element_type=F32
            ).astype(BF16)
            for r in range(4):
                outs[4 * k + r][...] = branch[r * share : (r + 1) * share]

    block = jax.ShapeDtypeStruct((share, width // 2), BF16)
    out_shapes = [jax.ShapeDtypeStruct((tokens, hidden), BF16), *[block] * 8]
    activated, *blocks = pl.pallas_call(
        kernel,
        grid=(1,),
        in_specs=[
            pl.BlockSpec(rows.shape, lambda i: (0, 0)),
            *(pl.BlockSpec(memory_space=pltpu.HBM) for _ in pieces),
        ],
        out_specs=[pl.BlockSpec(o.shape, lambda i: (0, 0)) for o in out_shapes],
        out_shape=out_shapes,
        scratch_shapes=[
            pltpu.VMEM((width, columns), BF16),
            pltpu.VMEM((tokens, lanes), BF16),
            pltpu.SemaphoreType.DMA((count,)),
        ],
        compiler_params=pltpu.CompilerParams(vmem_limit_bytes=58 * 2**20),
    )(rows, *pieces)
    return activated, blocks[:4], blocks[4:]


def teacher_parts(rows, gain, weight, positions):
    each = rows.shape[0] // EP_LEN
    share = rows.shape[0] // 4
    sizes = (share, share, share // 2, share // 2, share)

    def kernel(positions_ref, rows_ref, gain_ref, weight_ref, *rest):
        outs, scaled = rest[:-1], rest[-1]
        for k in range(EP_LEN):
            low = pl.multiple_of(positions_ref[k] * each, each)
            wide = rows_ref[pl.ds(low, each), :].astype(F32)
            scaled[k * each : (k + 1) * each, :] = (wide * gain_ref[...]).astype(BF16)
        product = jnp.dot(scaled[...], weight_ref[...], preferred_element_type=F32).astype(BF16)
        low = 0
        for out, size in zip(outs, sizes):
            out[...] = product[low : low + size]
            low += size

    return pl.pallas_call(
        kernel,
        in_specs=[
            pl.BlockSpec(memory_space=pltpu.SMEM),
            *(pl.BlockSpec(memory_space=pltpu.VMEM) for _ in range(3)),
        ],
        out_specs=[pl.BlockSpec(memory_space=pltpu.VMEM) for _ in sizes],
        out_shape=[jax.ShapeDtypeStruct((size, weight.shape[1]), BF16) for size in sizes],
        scratch_shapes=[pltpu.VMEM(rows.shape, BF16)],
        compiler_params=pltpu.CompilerParams(vmem_limit_bytes=40 * 2**20),
    )(positions, rows, gain[None, :], weight)


def gather_z(rows):
    return jnp.concatenate([rows, *(exchange(rows, "z", k) for k in (1, 2, 3))], axis=0)


def added(parts, arrived):
    total = parts.astype(F32)
    for a in arrived:
        total = total + a.astype(F32)
    return total


def scatter_y(blocks):
    return added(blocks[0], [shift(blocks[k], "y", k) for k in (1, 2, 3)])


def scatter_z(parts):
    n = parts.shape[0] // 4
    return added(parts[:n], [exchange(parts[k * n : (k + 1) * n], "z", k) for k in (1, 2, 3)])


def scatter_z_halving(parts, *gates):
    n = parts.shape[0] // 4
    pair = added(parts[: 2 * n], [exchange(parts[2 * n :], "z", 2)])
    return added(pair[:n], [exchange(after(pair[n:].astype(BF16), *gates), "z", 1)])


def scatter_ring(own, first, top, bottom, third, axis, *gates):
    half = top.shape[0]
    top, bottom = shift(top, axis, 1), shift(bottom, axis, -1)
    up = jnp.concatenate([first[:half] + top, first[half:]], axis=0)
    down = jnp.concatenate([third[:half], third[half:] + bottom], axis=0)
    up, down = after(up, *gates), after(down, *gates)
    return added(own, [shift(up, axis, 1), shift(down, axis, -1)]), (top, bottom)


def two_parts(values):
    high = lax.reduce_precision(values, 8, 7)
    both = jnp.concatenate([high, values - high], axis=1).astype(BF16)
    return jnp.pad(both, ((0, 0), (0, 128 - both.shape[1])))


def pick(onehot, rows):
    return jnp.dot(onehot.astype(BF16), rows, preferred_element_type=F32).astype(BF16)


def to_owners(rows, owner_local, gate):
    owner = owner_local[:, 0]
    index = jnp.arange(owner.shape[0], dtype=jnp.int32)
    earlier = (owner[None, :] == owner[:, None]) & (index[None, :] < index[:, None])
    rank = jnp.sum(earlier.astype(jnp.int32), axis=1)
    g, x, c = (lax.axis_index(a) for a in OWNERS)
    to_c = (owner % 2 + c) % 2
    to_g = (owner // 8 + g) % 2
    to_x = (owner // 2 % 4 - x) % 4
    place = (to_g * 4 + to_x) * 2 + rank
    slots = jnp.arange(16, dtype=jnp.int32)[:, None]
    stay = pick((slots == place[None, :]) & (to_c[None, :] == 0), rows)
    leave = pick((slots == place[None, :]) & (to_c[None, :] == 1), rows)
    arrived = shift(leave, "core", 1)
    kept = jnp.concatenate([stay[:8], arrived[:8]], axis=0)
    sent = after(jnp.concatenate([stay[8:], arrived[8:]], axis=0), gate)
    both = jnp.concatenate([kept, shift(sent, "group", 1)], axis=0)
    place = jnp.arange(32, dtype=jnp.int32)
    by_x = pick((place // 2 % 4 * 4 + place // 8) * 2 + place % 2 == place[:, None], both)
    groups = [by_x[8 * k : 8 * (k + 1)] for k in range(4)]
    here = jnp.concatenate([groups[0], *(shift(groups[k], "x", k) for k in (1, 2, 3))], axis=0)
    source = jnp.arange(32, dtype=jnp.int32)
    k, sg, sc, r = source // 8, source // 4 % 2, source // 2 % 2, source % 2
    final = (((g + sg) % 2 * 4 + (x - k) % 4) * 2 + (c + sc) % 2) * 2 + r
    return pick(jnp.arange(32, dtype=jnp.int32)[:, None] == final[None, :], here)


def local(
    teacher_hidden,
    teacher_gain,
    project_weight,
    student_hidden,
    student_gain,
    gate_weight,
    up_weight,
    down_weight,
    owner_map,
    token_ids,
    token_counts,
    id_weight,
):
    episodes = token_counts.shape[0]
    hidden = gate_weight.shape[1]
    width = student_hidden.shape[1]
    block = width // 4
    position = lax.axis_index(TENSOR)
    tokens_all = EP_LEN * episodes * lax.axis_size(OWNERS)

    near = jnp.concatenate([down_weight.T, gate_weight, up_weight], axis=1)
    rows_each = near.shape[0]
    near_far = shift(near, "group", 1)
    ahead = jnp.arange(EP_LEN, dtype=jnp.int32)
    positions = (lax.axis_index("z") ^ ahead % 4) * 4 + (lax.axis_index("y") + ahead // 4) % 4
    near_across = shift(near, "core", 1)
    rows = after(teacher_hidden, near_across)
    parts = teacher_parts(rows, teacher_gain, project_weight, positions)
    near_own = ring_pieces(near, "x", parts[0])
    near_first, near_last = (near_own[1], near_own[4]), (near_own[2], near_own[3])
    parts = [after(p, *near_last) for p in parts]
    near_other = [near_across, *swapped(near_own[1:])]
    student_hidden, teacher_hidden = after(student_hidden, near), after(teacher_hidden, near)
    wide = student_hidden.astype(F32)
    rescale = lax.rsqrt(jnp.mean(wide * wide, axis=1, keepdims=True) + EPSILON)
    normed = (wide * rescale * student_gain[None, :]).astype(BF16)
    both_rows = relative_columns(jnp.concatenate([normed, student_hidden], axis=0))
    student = both_rows[episodes:].astype(F32)
    widened = teacher_hidden.astype(F32)
    squares = jnp.sum(widened * widened, axis=1).reshape(EP_LEN, episodes).T
    column = jnp.concatenate([both_rows[:episodes], two_parts(squares)], axis=1)
    column = after(column, near_far, *near_other)
    pair = jnp.concatenate([column, exchange(column, "z", 1)], axis=0)
    column = jnp.concatenate([pair, exchange(pair, "z", 2)], axis=0)
    far_own = ring_pieces(after(near_far, pair), "x")
    far_first = (far_own[1], far_own[4])
    ahead, top, bottom, behind = far_own[1:]
    far_other = swapped([far_own[0], after(ahead, top, bottom), top, bottom, after(behind, top, bottom)])
    gathered_pieces = ring_pieces(after(column, *far_first, far_other[0]), "y", far_other[1], far_other[4])
    gathered = jnp.concatenate(gathered_pieces, axis=0)
    totals = jnp.sum(gathered[:, width:].reshape(EP_LEN, episodes, -1).astype(F32), axis=0)
    totals = totals[:, :EP_LEN] + totals[:, EP_LEN : 2 * EP_LEN]
    totals = jnp.sum(jnp.where(jnp.arange(EP_LEN)[None, :] == position, totals, 0.0), axis=1)
    inverse = lax.rsqrt(totals / DT + EPSILON)

    total, _ = scatter_ring(*parts, "y")
    total = scatter_z_halving(after(total.astype(BF16), column))
    projected = (total * inverse[:, None]).astype(BF16)
    projected = relative_columns(projected).astype(F32)

    ids = jnp.arange(id_weight.shape[0], dtype=jnp.int32)
    looked = jnp.sum(jnp.where(token_ids[:, None] == ids[None, :], id_weight[None, :], 0.0), axis=1)
    weight = jnp.where(position < token_counts, looked, 0.0).astype(BF16).astype(F32)
    scale = 1.0 / math.sqrt(tokens_all)

    def starts(pieces, low):
        return ring_starts(pieces, rows_each, low) + ring_starts(pieces, rows_each, low + block)

    activated, near_branch, far_branch = feed_forward(
        after(gathered, total),
        near_own + near_other + far_own + far_other,
        starts(near_own, 0) + starts(far_own, 2 * block),
        hidden,
    )

    def gradient_half(far, branch_rows):
        columns = slice(far * 2 * block, (far + 1) * 2 * block)
        predicted = student[:, columns] + scatter_z(branch_rows)
        difference = predicted - projected[:, columns]
        return predicted, gather_z((weight[:, None] * difference * scale).astype(BF16))

    def owners_half(grad):
        mine, other = (
            jnp.einsum(
                "rc,rh->ch", grad[:, a : a + block], activated, preferred_element_type=F32
            ).astype(BF16)
            for a in (0, block)
        )
        both = mine + shift(other, "core", 1)
        quarter = block // 4
        own, first, second, third = (both[k * quarter : (k + 1) * quarter] for k in range(4))
        return own, first, second[: quarter // 2], second[quarter // 2 :], third

    far_rows = scatter_y(far_branch).astype(BF16)
    near_rows = scatter_y(near_branch).astype(BF16)
    far_predicted, far_column = gradient_half(1, far_rows)
    near_predicted, near_column = gradient_half(0, near_rows)
    far_ring, near_ring = ring_pieces(far_column, "y"), ring_pieces(near_column, "y")
    far_grad, near_grad = jnp.concatenate(far_ring, axis=0), jnp.concatenate(near_ring, axis=0)
    far_reduced, far_arrived = scatter_ring(*owners_half(far_grad), "x")
    far_reduced = far_reduced.astype(BF16)
    own, first, top, bottom, third = owners_half(near_grad)
    top, bottom = after(top, *far_arrived), after(bottom, *far_arrived)
    near_reduced, _ = scatter_ring(own, first, top, bottom, third, "x", far_reduced)
    down_grad = near_reduced + shift(far_reduced, "group", 1).astype(F32)

    predicted = [near_predicted, far_predicted]
    rows = jnp.concatenate([p.astype(BF16) for p in predicted], axis=1)
    student_out = to_owners(absolute_columns(rows), owner_map, far_arrived[0])
    return (student_out[None, None], down_grad)


def solution(mesh):
    split = Mesh(mesh.devices.reshape(*AXES.values()), tuple(AXES))
    placed = (
        P(OWNERS, TENSOR),
        P(TENSOR),
        P(TENSOR, None),
        P((*OWNERS, *TENSOR), None),
        P(),
        P(OWNERS, TENSOR),
        P(OWNERS, TENSOR),
        P(TENSOR, OWNERS),
        P(OWNERS, None),
        P((*OWNERS, *TENSOR)),
        P(OWNERS),
        P(),
    )
    return jax.shard_map(
        local,
        mesh=split,
        in_specs=placed,
        out_specs=(P(OWNERS, TENSOR, None, None), P(OWNERS, TENSOR)),
        check_vma=False,
    )
```
